32 devices in a mesh: dp: 4 (over y, core), mp: 8 (over z, x).
Axes of the slice: x: 2, y: 2, z: 4, core: 2. Of those that a mesh axis runs over, the one named last changes fastest.
Arguments:
- grad_partials: bfloat16 [4, 16, 512, 512], P('dp', 'mp')
- owner_lists: int32 [16], replicated, may hold values from 0 to 15, as said below
- owner_offsets: int32 [9], replicated, may hold values from 0 to 16, as said below
- left_roots: bfloat16 [8, 4, 512, 512], P('mp', 'dp')
- right_roots: bfloat16 [8, 4, 512, 512], P('mp', 'dp')
Outputs:
- update: bfloat16 [16, 512, 512], P('mp', 'dp')
The draws below stay inside these ranges and needn't reach their ends.
Inputs may be any that keep to these rules, and one draw needn't show every extreme that they name: `owner_lists`: a permutation of the block numbers; no owner column owns two blocks of one mp shard (blocks j * 2 to j * 2 + 1). `owner_offsets`: begins with 0, ends with 16, never falls; every owner column owns 1 to 4 blocks, and some column exactly 4.
All inputs are finite; a program needn't handle non-finite values.
Results may differ from the reference program's by a relative error of at most 0.025.
Values may be sent and summed in bfloat16 or wider, within the bound.
No kernel may reach another device: no remote copies, remote signals or barrier semaphores. Data moves between devices by JAX's collectives and lax.ppermute only.
A program may use at most 64 MiB of HBM per device.

```python
import math
import jax
import jax.numpy as jnp
from jax import lax

BLOCK = 512
BLK_DEV = 2
BLOCKS = 16
N_DP = 4
N_MP = 8


def ownership(key):
    key = jax.random.fold_in(key, 5)
    first_key, second_key, third_key = jax.random.split(key, 3)
    column_order = jax.random.permutation(first_key, N_MP)
    needed = N_DP - BLK_DEV
    ranks = jnp.arange(N_MP, dtype=jnp.int32)
    given = jnp.clip(needed - (ranks - 1) * (BLK_DEV - 1), 0, BLK_DEV - 1)
    ranked_counts = jnp.where(ranks == 0, N_DP, BLK_DEV - given).astype(jnp.int32)
    counts = jnp.zeros((N_MP,), jnp.int32).at[column_order].set(ranked_counts)
    offsets = jnp.concatenate([jnp.zeros((1,), jnp.int32), jnp.cumsum(counts).astype(jnp.int32)])
    rotation = jax.random.randint(second_key, (), 0, BLOCKS)
    shard_order = jax.random.permutation(third_key, N_MP)
    sequence = (jnp.arange(BLOCKS, dtype=jnp.int32) + rotation) % BLOCKS
    levels = sequence // N_MP
    shards = shard_order[sequence % N_MP]
    lists = (shards * BLK_DEV + levels).astype(jnp.int32)
    return (lists, offsets)


def draw_owner_lists(key, part):
    lists, offsets = ownership(key)
    return lists


def draw_owner_offsets(key, part):
    lists, offsets = ownership(key)
    return offsets


def draw_grad_partials(key, part):
    key = jax.random.fold_in(key, 11)
    row_key, col_key, noise_key = jax.random.split(key, 3)
    row_scale = jnp.exp(jax.random.uniform(row_key, (BLOCKS, BLOCK, 1)) * math.log(10.0))
    col_scale = jnp.exp(jax.random.uniform(col_key, (BLOCKS, 1, BLOCK)) * math.log(10.0))
    rising = (1.0 + 2.0 * jnp.arange(BLOCKS, dtype=jnp.float32) / max(BLOCKS - 1, 1)).reshape(BLOCKS, 1, 1)
    row_place = (jnp.arange(BLOCK, dtype=jnp.float32) / max(BLOCK - 1, 1)).reshape(1, BLOCK, 1)
    noise = jax.random.normal(noise_key, (N_DP, BLOCKS, BLOCK, BLOCK))
    factor = 0.1
    row_rise = 1.0 + 2.0 * row_place
    return (factor * rising * row_rise * row_scale * col_scale * noise).astype(jnp.bfloat16)


def symmetric_root(key, diag_low, diag_high):
    off_key, diag_key = jax.random.split(key)
    spread = 0.9 / math.sqrt(BLOCK)
    offdiag = jax.random.uniform(off_key, (N_MP, N_DP, BLOCK, BLOCK), minval=-spread, maxval=spread)
    offdiag = 0.5 * (offdiag + jnp.swapaxes(offdiag, -1, -2))
    diagonal = jax.random.uniform(diag_key, (N_MP, N_DP, BLOCK, 1), minval=diag_low, maxval=diag_high)
    identity = (jnp.arange(BLOCK)[:, None] == jnp.arange(BLOCK)[None, :]).astype(jnp.float32)
    return (offdiag + diagonal * identity).astype(jnp.bfloat16)


def draw_left_roots(key, part):
    key = jax.random.fold_in(key, 21)
    return symmetric_root(key, 1.0, 2.0)


def draw_right_roots(key, part):
    key = jax.random.fold_in(key, 22)
    return symmetric_root(key, 1.0, 2.0)


def setup_inputs(seed: int = 0) -> dict:
    key_list = jax.random.split(jax.random.key(seed), 6)
    grad_partials = draw_grad_partials(jax.random.fold_in(key_list[5], 71), 0)
    owner_lists = draw_owner_lists(jax.random.fold_in(key_list[5], 71), 0)
    owner_offsets = draw_owner_offsets(jax.random.fold_in(key_list[5], 71), 0)
    left_roots = draw_left_roots(jax.random.fold_in(key_list[5], 71), 0)
    right_roots = draw_right_roots(jax.random.fold_in(key_list[5], 71), 0)
    return {"grad_partials": grad_partials, "owner_lists": owner_lists, "owner_offsets": owner_offsets, "left_roots": left_roots, "right_roots": right_roots}


epsilon = 1e-06
max_rms = 1.0

def reference(grad_partials, owner_lists, owner_offsets, left_roots, right_roots):
    grad = grad_partials[0].astype(jnp.float32)
    for replica in range(1, N_DP):
        grad = grad + grad_partials[replica].astype(jnp.float32)
    grad_b = grad.astype(jnp.bfloat16)
    grad_sq = grad_b.astype(jnp.float32)
    square_total = jnp.sum(grad_sq * grad_sq)
    clip_factor = max_rms / jnp.sqrt(square_total / (BLOCKS * BLOCK * BLOCK) + epsilon)
    positions = jnp.arange(BLOCKS, dtype=jnp.int32)
    owner_column = lax.optimization_barrier(jnp.sum((owner_offsets[1:][None, :] <= positions[:, None]).astype(jnp.int32), axis=1)).astype(jnp.int32)
    owner_slot = (positions - owner_offsets[owner_column]).astype(jnp.int32)

    def precondition(position):
        block_id = owner_lists[position]
        whole_block = grad_b[block_id]
        left_factor = left_roots[owner_column[position], owner_slot[position]]
        right_factor = right_roots[owner_column[position], owner_slot[position]]
        right_prod = jnp.dot(whole_block, right_factor, preferred_element_type=jnp.float32).astype(jnp.bfloat16)
        precond = jnp.dot(left_factor, right_prod, preferred_element_type=jnp.float32)
        block_f = whole_block.astype(jnp.float32)
        graft_scale = jnp.sqrt(jnp.mean(block_f * block_f) + epsilon) / jnp.sqrt(jnp.mean(precond * precond) + epsilon)
        return (clip_factor * graft_scale * precond).astype(jnp.bfloat16)
    results = lax.map(precondition, positions)
    update = jnp.zeros((BLOCKS, BLOCK, BLOCK), jnp.bfloat16).at[owner_lists].set(results)
    return update
```

```python
import functools

import jax
import jax.numpy as jnp
from jax import lax
from jax.experimental import pallas as pl
from jax.experimental.pallas import tpu as pltpu
from jax.sharding import PartitionSpec as P

epsilon = 1e-06
max_rms = 1.0

SMEM = pl.BlockSpec(memory_space=pltpu.SMEM)
VMEM = pl.BlockSpec(memory_space=pltpu.VMEM)


def swap(value, axis, distance):
    count = lax.axis_size(axis)
    return lax.ppermute(value, axis, [(i, i ^ distance) for i in range(count)])


def add_rounded(a, b):
    return (a.astype(jnp.float32) + b.astype(jnp.float32)).astype(jnp.bfloat16)


def core_sum(partial_blocks, dp_index):
    half = partial_blocks.shape[1] // 2
    core = dp_index % 2
    kept = lax.dynamic_slice_in_dim(partial_blocks, core * half, half, axis=1)
    given = lax.dynamic_slice_in_dim(partial_blocks, (1 - core) * half, half, axis=1)
    return add_rounded(kept, swap(given, "dp", 1))


def chip_sum(total, dp_count):
    distance = 2
    while distance < dp_count:
        total = add_rounded(total, swap(total, "dp", distance))
        distance *= 2
    return total


def both_halves(total, dp_index):
    core = dp_index % 2
    other = swap(total, "dp", 1)
    low = jnp.where(core == 0, total, other)
    high = jnp.where(core == 0, other, total)
    return jnp.concatenate([low, high], axis=1)


def gather_rows(rows, dp_count, dp_index):
    per_shard, _, width = rows.shape
    parts = rows[:, None]
    distance = dp_count // 2
    while distance >= 1:
        other = swap(parts, "dp", distance)
        bit = (dp_index // distance) % 2
        low = jnp.where(bit == 0, parts, other)
        high = jnp.where(bit == 0, other, parts)
        parts = jnp.stack([low, high], axis=2)
        parts = parts.reshape(per_shard, -1, *rows.shape[1:])
        distance //= 2
    return parts.reshape(per_shard, -1, width)


def plan_routes(mp_count, per_shard, lists, offsets, plan):
    column = lax.axis_index("mp")
    start = offsets[column]
    for j in range(mp_count):
        plan[j] = 0

    def note(p, carry):
        plan[lists[p] // per_shard] = p - start
        return carry

    lax.fori_loop(start, offsets[column + 1], note, 0)

    def owner(p, carry):
        block = lists[p]

        @pl.when(block // per_shard == column)
        def _():
            plan[mp_count + block % per_shard] = lax.fori_loop(
                0, mp_count, lambda c, total: total + (offsets[c + 1] <= p).astype(jnp.int32), 0
            )

        return carry

    lax.fori_loop(0, lists.shape[0], owner, 0)


def right_kernel(mp_count, per_shard, lists, offsets, slots, plan, out):
    plan_routes(mp_count, per_shard, lists, offsets, plan)
    for j in range(mp_count):
        out[j] = slots[plan[j]]


def split_kernel(dp_count, factor, *outs):
    rows = outs[0].shape[0]
    me = lax.axis_index("dp")
    for d in range(1, dp_count):
        outs[d - 1][...] = factor[0, 0, pl.ds(pl.multiple_of((me ^ d) * rows, rows), rows), :]


def left_kernel(mp_count, dp_count, plan, factor, half_sq, *refs):
    pieces, out, slots = refs[: dp_count - 1], refs[dp_count - 1], refs[dp_count]
    rows, width = slots.shape[1:]
    lanes = out.shape[2]
    me = lax.axis_index("dp")
    slots[me] = factor[0, 0, pl.ds(pl.multiple_of(me * rows, rows), rows), :]
    for d in range(1, dp_count):
        slots[me ^ d] = pieces[d - 1][...]
    total = jnp.sum(half_sq[...], axis=0, keepdims=True)
    first = total.astype(jnp.bfloat16).astype(jnp.float32)
    second = (total - first).astype(jnp.bfloat16).astype(jnp.float32)
    third = total - first - second
    row = lax.broadcasted_iota(jnp.int32, (16, lanes), 0)
    parts = jnp.where(row == 0, first, jnp.where(row == 1, second, jnp.where(row == 2, third, 0.0)))
    parts = parts.astype(jnp.bfloat16)
    for j in range(mp_count):
        slot = plan[j]
        for c in range(width // lanes):
            out[j, c * rows : (c + 1) * rows, :] = slots[slot, :, c * lanes : (c + 1) * lanes]
        out[j, out.shape[1] - 16 :, :] = parts


def pick_kernel(mp_count, per_shard, plan, arrived, out):
    for r in range(per_shard):
        out[r] = arrived[plan[mp_count + r]]


def precond_kernel(mp_count, per_shard, plan, right_prod, half_sq, arrived, precond, stats, left):
    rows, lanes = left.shape[0], arrived.shape[2]
    stats[...] = jnp.zeros_like(stats)
    stats[per_shard : 2 * per_shard, :] = half_sq[...]
    parts = jnp.sum(arrived[:, arrived.shape[1] - 16 :, :].astype(jnp.float32), axis=0)
    stats[2 * per_shard : 2 * per_shard + 1, :] = jnp.sum(parts, axis=0, keepdims=True)
    for r in range(per_shard):
        source = plan[mp_count + r]
        for c in range(left.shape[1] // lanes):
            left[:, c * lanes : (c + 1) * lanes] = arrived[source, c * rows : (c + 1) * rows, :]
        product = jnp.dot(left[...], right_prod[r], preferred_element_type=jnp.float32)
        precond[r] = product
        total = jnp.sum(jnp.sum(product * product, axis=1, keepdims=True), axis=0, keepdims=True)
        stats[r : r + 1, :] = jnp.broadcast_to(total, (1, lanes))


def finish_kernel(area, cells, precond, *refs):
    parts, update = refs[:-1], refs[-1]
    per_shard = update.shape[0]
    total = parts[0][...]
    for part in parts[1:]:
        total += part[...]
    precond_sq, block_sq = total[:per_shard], total[per_shard : 2 * per_shard]
    square_total = total[2 * per_shard : 2 * per_shard + 1]
    graft = jnp.sqrt(block_sq / area + epsilon) / jnp.sqrt(precond_sq / area + epsilon)
    scale = max_rms / jnp.sqrt(square_total / cells + epsilon) * graft
    for r in range(per_shard):
        update[r] = (scale[r : r + 1, :1] * precond[r]).astype(update.dtype)


def shards(grad_partials, owner_lists, owner_offsets, left_roots, right_roots):
    dp_count = lax.axis_size("dp")
    mp_count = lax.axis_size("mp")
    dp_index = lax.axis_index("dp")
    partial_blocks = grad_partials[0]
    per_shard = partial_blocks.shape[0]
    width = partial_blocks.shape[2]
    rows = width // dp_count
    area = width * width
    cells = owner_lists.shape[0] * area
    piece = jax.ShapeDtypeStruct((rows, width), jnp.bfloat16)
    lanes = 128

    params = pltpu.CompilerParams(vmem_limit_bytes=16 * 2**20)

    def over(rows_out, axis):
        return lax.all_to_all(rows_out, axis, split_axis=0, concat_axis=0, tiled=True)

    right_slots = over(right_roots[0, 0].reshape(dp_count, rows, width), "dp")
    total = core_sum(partial_blocks, dp_index)
    right_slots, total = lax.optimization_barrier((right_slots, total))
    plan, outgoing = pl.pallas_call(
        functools.partial(right_kernel, mp_count, per_shard),
        out_shape=[
            jax.ShapeDtypeStruct((mp_count + per_shard,), jnp.int32),
            jax.ShapeDtypeStruct((mp_count, rows, width), jnp.bfloat16),
        ],
        in_specs=[SMEM, SMEM, VMEM],
        out_specs=[SMEM, VMEM],
        compiler_params=params,
    )(owner_lists, owner_offsets, right_slots)
    right_arrived = over(outgoing, "mp")
    given = pl.pallas_call(
        functools.partial(split_kernel, dp_count),
        out_shape=[piece] * (dp_count - 1),
        in_specs=[VMEM],
        out_specs=[VMEM] * (dp_count - 1),
        compiler_params=params,
    )(left_roots)
    taken = [swap(given[d - 1], "dp", d) for d in range(1, dp_count)]
    total = chip_sum(total, dp_count)
    total_f = total.astype(jnp.float32)
    half_sq = jnp.broadcast_to(
        (jnp.sum(total_f * total_f, axis=(1, 2)) * (2 / dp_count)).reshape(per_shard, 1),
        (per_shard, lanes),
    )
    left_outgoing = pl.pallas_call(
        functools.partial(left_kernel, mp_count, dp_count),
        out_shape=jax.ShapeDtypeStruct((mp_count, rows * width // lanes + 16, lanes), jnp.bfloat16),
        in_specs=[SMEM, VMEM, VMEM] + [VMEM] * (dp_count - 1),
        out_specs=VMEM,
        scratch_shapes=[pltpu.VMEM((dp_count, rows, width), jnp.bfloat16)],
        compiler_params=params,
    )(plan, left_roots, half_sq, *taken)
    left_arrived = over(left_outgoing, "mp")
    right_rows = pl.pallas_call(
        functools.partial(pick_kernel, mp_count, per_shard),
        out_shape=jax.ShapeDtypeStruct((per_shard, rows, width), jnp.bfloat16),
        in_specs=[SMEM, VMEM],
        out_specs=VMEM,
        compiler_params=params,
    )(plan, right_arrived)
    right = gather_rows(right_rows, dp_count, dp_index)

    grad = both_halves(total, dp_index)
    right_prod = jnp.einsum(
        "bij,bjk->bik", grad, right, preferred_element_type=jnp.float32
    ).astype(jnp.bfloat16)
    precond, stats = pl.pallas_call(
        functools.partial(precond_kernel, mp_count, per_shard),
        out_shape=[
            jax.ShapeDtypeStruct((per_shard, rows, width), jnp.float32),
            jax.ShapeDtypeStruct((pl.cdiv(2 * per_shard + 1, 8) * 8, lanes), jnp.float32),
        ],
        in_specs=[SMEM, VMEM, VMEM, VMEM],
        out_specs=[VMEM, VMEM],
        scratch_shapes=[pltpu.VMEM((rows, width), jnp.bfloat16)],
        compiler_params=params,
    )(plan, right_prod, half_sq, left_arrived)
    parts = [stats] + [swap(stats, "dp", d) for d in range(1, dp_count)]
    return pl.pallas_call(
        functools.partial(finish_kernel, area, cells),
        out_shape=jax.ShapeDtypeStruct((per_shard, rows, width), jnp.bfloat16),
        in_specs=[VMEM] * (1 + dp_count),
        out_specs=VMEM,
        compiler_params=params,
    )(precond, *parts)


def solution(mesh):
    return jax.shard_map(
        shards,
        mesh=mesh,
        in_specs=(
            P("dp", "mp", None, None),
            P(),
            P(),
            P("mp", "dp", None, None),
            P("mp", "dp", None, None),
        ),
        out_specs=P("mp", "dp", None),
        check_vma=False,
    )
```

```python
import functools

import jax
import jax.numpy as jnp
from jax import lax
from jax.experimental import pallas as pl
from jax.experimental.pallas import tpu as pltpu
from jax.sharding import PartitionSpec as P

epsilon = 1e-06
max_rms = 1.0

SMEM = pl.BlockSpec(memory_space=pltpu.SMEM)
VMEM = pl.BlockSpec(memory_space=pltpu.VMEM)
ANY = pl.BlockSpec(memory_space=pl.ANY)


def swap(value, axis, distance):
    count = lax.axis_size(axis)
    return lax.ppermute(value, axis, [(i, i ^ distance) for i in range(count)])


def add_rounded(a, b):
    return (a.astype(jnp.float32) + b.astype(jnp.float32)).astype(jnp.bfloat16)


def core_sum(partial_blocks, dp_index):
    half = partial_blocks.shape[1] // 2
    core = dp_index % 2
    kept = lax.dynamic_slice_in_dim(partial_blocks, core * half, half, axis=1)
    given = lax.dynamic_slice_in_dim(partial_blocks, (1 - core) * half, half, axis=1)
    return add_rounded(kept, swap(given, "dp", 1))


def chip_sum(total, dp_count):
    distance = 2
    while distance < dp_count:
        total = add_rounded(total, swap(total, "dp", distance))
        distance *= 2
    return total


def both_halves(total, dp_index):
    core = dp_index % 2
    other = swap(total, "dp", 1)
    low = jnp.where(core == 0, total, other)
    high = jnp.where(core == 0, other, total)
    return jnp.concatenate([low, high], axis=1)


def gather_rows(rows, dp_count, dp_index):
    per_shard, _, width = rows.shape
    parts = rows[:, None]
    distance = dp_count // 2
    while distance >= 1:
        other = swap(parts, "dp", distance)
        bit = (dp_index // distance) % 2
        low = jnp.where(bit == 0, parts, other)
        high = jnp.where(bit == 0, other, parts)
        parts = jnp.stack([low, high], axis=2)
        parts = parts.reshape(per_shard, -1, *rows.shape[1:])
        distance //= 2
    return parts.reshape(per_shard, -1, width)


def plan_kernel(mp_count, per_shard, lists, offsets, plan):
    column = lax.axis_index("mp")
    start = offsets[column]
    for j in range(mp_count):
        plan[j] = 0

    def note(p, carry):
        plan[lists[p] // per_shard] = p - start
        return carry

    lax.fori_loop(start, offsets[column + 1], note, 0)

    def owner(p, carry):
        block = lists[p]

        @pl.when(block // per_shard == column)
        def _():
            plan[mp_count + block % per_shard] = lax.fori_loop(
                0, mp_count, lambda c, total: total + (offsets[c + 1] <= p).astype(jnp.int32), 0
            )

        return carry

    lax.fori_loop(0, lists.shape[0], owner, 0)


def right_kernel(mp_count, plan, slots, *outs):
    column = lax.axis_index("mp")
    for d in range(mp_count):
        outs[d][...] = slots[plan[column ^ d]]


def split_kernel(dp_count, factor, *outs):
    rows = outs[0].shape[0]
    me = lax.axis_index("dp")
    for d in range(1, dp_count):
        outs[d - 1][...] = factor[0, 0, pl.ds(pl.multiple_of((me ^ d) * rows, rows), rows), :]


def left_kernel(mp_count, dp_count, plan, factor, half_sq, *refs):
    pieces, out, slots = refs[: dp_count - 1], refs[dp_count - 1], refs[dp_count]
    rows, width = slots.shape[1:]
    lanes = out.shape[2]
    me = lax.axis_index("dp")
    slots[me] = factor[0, 0, pl.ds(pl.multiple_of(me * rows, rows), rows), :]
    for d in range(1, dp_count):
        slots[me ^ d] = pieces[d - 1][...]
    total = jnp.sum(half_sq[...], axis=0, keepdims=True)
    first = total.astype(jnp.bfloat16).astype(jnp.float32)
    second = (total - first).astype(jnp.bfloat16).astype(jnp.float32)
    third = total - first - second
    row = lax.broadcasted_iota(jnp.int32, (16, lanes), 0)
    parts = jnp.where(row == 0, first, jnp.where(row == 1, second, jnp.where(row == 2, third, 0.0)))
    parts = parts.astype(jnp.bfloat16)
    for j in range(mp_count):
        slot = plan[j]
        for c in range(width // lanes):
            out[j, c * rows : (c + 1) * rows, :] = slots[slot, :, c * lanes : (c + 1) * lanes]
        out[j, out.shape[1] - 16 :, :] = parts


def pick_kernel(mp_count, per_shard, plan, *refs):
    arrived, out = refs[:mp_count], refs[-1]
    shard = lax.axis_index("mp")
    for r in range(per_shard):
        source = plan[mp_count + r] ^ shard
        for d in range(mp_count):

            @pl.when(source == d)
            def _(d=d, r=r):
                out[r] = arrived[d][...]


def precond_kernel(mp_count, per_shard, plan, right_prod, half_sq, arrived, precond, stats, left):
    rows, lanes = left.shape[0], arrived.shape[2]
    stats[...] = jnp.zeros_like(stats)
    stats[per_shard : 2 * per_shard, :] = half_sq[...]
    parts = jnp.sum(arrived[:, arrived.shape[1] - 16 :, :].astype(jnp.float32), axis=0)
    stats[2 * per_shard : 2 * per_shard + 1, :] = jnp.sum(parts, axis=0, keepdims=True)
    for r in range(per_shard):
        source = plan[mp_count + r]
        for c in range(left.shape[1] // lanes):
            left[:, c * lanes : (c + 1) * lanes] = arrived[source, c * rows : (c + 1) * rows, :]
        product = jnp.dot(left[...], right_prod[r], preferred_element_type=jnp.float32)
        precond[r] = product
        total = jnp.sum(jnp.sum(product * product, axis=1, keepdims=True), axis=0, keepdims=True)
        stats[r : r + 1, :] = jnp.broadcast_to(total, (1, lanes))


def finish_kernel(area, cells, precond, *refs):
    parts, update = refs[:-1], refs[-1]
    per_shard = update.shape[0]
    total = parts[0][...]
    for part in parts[1:]:
        total += part[...]
    precond_sq, block_sq = total[:per_shard], total[per_shard : 2 * per_shard]
    square_total = total[2 * per_shard : 2 * per_shard + 1]
    graft = jnp.sqrt(block_sq / area + epsilon) / jnp.sqrt(precond_sq / area + epsilon)
    scale = max_rms / jnp.sqrt(square_total / cells + epsilon) * graft
    for r in range(per_shard):
        update[r] = (scale[r : r + 1, :1] * precond[r]).astype(update.dtype)


def shards(grad_partials, owner_lists, owner_offsets, left_roots, right_roots):
    dp_count = lax.axis_size("dp")
    mp_count = lax.axis_size("mp")
    dp_index = lax.axis_index("dp")
    partial_blocks = grad_partials[0]
    per_shard = partial_blocks.shape[0]
    width = partial_blocks.shape[2]
    rows = width // dp_count
    area = width * width
    cells = owner_lists.shape[0] * area
    piece = jax.ShapeDtypeStruct((rows, width), jnp.bfloat16)
    lanes = 128

    params = pltpu.CompilerParams(vmem_limit_bytes=16 * 2**20)

    def over_dp(factor):
        return lax.all_to_all(
            factor[0, 0].reshape(dp_count, rows, width), "dp", split_axis=0, concat_axis=0, tiled=True
        )

    plan = pl.pallas_call(
        functools.partial(plan_kernel, mp_count, per_shard),
        out_shape=jax.ShapeDtypeStruct((mp_count + per_shard,), jnp.int32),
        in_specs=[SMEM, SMEM],
        out_specs=SMEM,
        compiler_params=params,
    )(owner_lists, owner_offsets)
    right_slots = over_dp(right_roots)
    total = core_sum(partial_blocks, dp_index)
    right_slots, total, left_roots = lax.optimization_barrier((right_slots, total, left_roots))
    outgoing = pl.pallas_call(
        functools.partial(right_kernel, mp_count),
        out_shape=[piece] * mp_count,
        in_specs=[SMEM, VMEM],
        out_specs=[VMEM] * mp_count,
        compiler_params=params,
    )(plan, right_slots)
    given = pl.pallas_call(
        functools.partial(split_kernel, dp_count),
        out_shape=[piece] * (dp_count - 1),
        in_specs=[VMEM],
        out_specs=[VMEM] * (dp_count - 1),
        compiler_params=params,
    )(left_roots)
    taken = [swap(given[d - 1], "dp", d) for d in range(1, dp_count)]
    right_arrived = [outgoing[0]] + [swap(outgoing[d], "mp", d) for d in range(1, mp_count)]
    total = chip_sum(total, dp_count)
    total_f = total.astype(jnp.float32)
    half_sq = jnp.broadcast_to(
        (jnp.sum(total_f * total_f, axis=(1, 2)) * (2 / dp_count)).reshape(per_shard, 1),
        (per_shard, lanes),
    )
    left_outgoing = pl.pallas_call(
        functools.partial(left_kernel, mp_count, dp_count),
        out_shape=jax.ShapeDtypeStruct((mp_count, rows * width // lanes + 16, lanes), jnp.bfloat16),
        in_specs=[SMEM, VMEM, VMEM] + [VMEM] * (dp_count - 1),
        out_specs=VMEM,
        scratch_shapes=[pltpu.VMEM((dp_count, rows, width), jnp.bfloat16)],
        compiler_params=params,
    )(plan, left_roots, half_sq, *taken)
    left_arrived = lax.all_to_all(left_outgoing, "mp", split_axis=0, concat_axis=0, tiled=True)
    right_rows = pl.pallas_call(
        functools.partial(pick_kernel, mp_count, per_shard),
        out_shape=jax.ShapeDtypeStruct((per_shard, rows, width), jnp.bfloat16),
        in_specs=[SMEM] + [VMEM] * mp_count + [ANY],
        out_specs=VMEM,
        compiler_params=params,
    )(plan, *right_arrived, left_outgoing)
    right = gather_rows(right_rows, dp_count, dp_index)

    grad = both_halves(total, dp_index)
    right_prod = jnp.einsum(
        "bij,bjk->bik", grad, right, preferred_element_type=jnp.float32
    ).astype(jnp.bfloat16)
    precond, stats = pl.pallas_call(
        functools.partial(precond_kernel, mp_count, per_shard),
        out_shape=[
            jax.ShapeDtypeStruct((per_shard, rows, width), jnp.float32),
            jax.ShapeDtypeStruct((pl.cdiv(2 * per_shard + 1, 8) * 8, lanes), jnp.float32),
        ],
        in_specs=[SMEM, VMEM, VMEM, VMEM],
        out_specs=[VMEM, VMEM],
        scratch_shapes=[pltpu.VMEM((rows, width), jnp.bfloat16)],
        compiler_params=params,
    )(plan, right_prod, half_sq, left_arrived)
    parts = [stats] + [swap(stats, "dp", d) for d in range(1, dp_count)]
    return pl.pallas_call(
        functools.partial(finish_kernel, area, cells),
        out_shape=jax.ShapeDtypeStruct((per_shard, rows, width), jnp.bfloat16),
        in_specs=[VMEM] * (1 + dp_count),
        out_specs=VMEM,
        compiler_params=params,
    )(precond, *parts)


def solution(mesh):
    return jax.shard_map(
        shards,
        mesh=mesh,
        in_specs=(
            P("dp", "mp", None, None),
            P(),
            P(),
            P("mp", "dp", None, None),
            P("mp", "dp", None, None),
        ),
        out_specs=P("mp", "dp", None),
        check_vma=False,
    )
```

```python
import functools

import jax
import jax.numpy as jnp
from jax import lax
from jax.experimental import pallas as pl
from jax.experimental.pallas import tpu as pltpu
from jax.sharding import PartitionSpec as P

epsilon = 1e-06
max_rms = 1.0

SMEM = pl.BlockSpec(memory_space=pltpu.SMEM)
VMEM = pl.BlockSpec(memory_space=pltpu.VMEM)
ANY = pl.BlockSpec(memory_space=pl.ANY)


def swap(value, axis, distance):
    count = lax.axis_size(axis)
    return lax.ppermute(value, axis, [(i, i ^ distance) for i in range(count)])


def add_rounded(a, b):
    return (a.astype(jnp.float32) + b.astype(jnp.float32)).astype(jnp.bfloat16)


def core_sum(partial_blocks, dp_index):
    half = partial_blocks.shape[1] // 2
    core = dp_index % 2
    kept = lax.dynamic_slice_in_dim(partial_blocks, core * half, half, axis=1)
    given = lax.dynamic_slice_in_dim(partial_blocks, (1 - core) * half, half, axis=1)
    return add_rounded(kept, swap(given, "dp", 1))


def chip_sum(total, dp_count):
    distance = 2
    while distance < dp_count:
        total = add_rounded(total, swap(total, "dp", distance))
        distance *= 2
    return total


def both_halves(total, dp_index):
    core = dp_index % 2
    other = swap(total, "dp", 1)
    low = jnp.where(core == 0, total, other)
    high = jnp.where(core == 0, other, total)
    return jnp.concatenate([low, high], axis=1)


def gather_rows(rows, dp_count, dp_index):
    per_shard, _, width = rows.shape
    parts = rows[:, None]
    distance = dp_count // 2
    while distance >= 1:
        other = swap(parts, "dp", distance)
        bit = (dp_index // distance) % 2
        low = jnp.where(bit == 0, parts, other)
        high = jnp.where(bit == 0, other, parts)
        parts = jnp.stack([low, high], axis=2)
        parts = parts.reshape(per_shard, -1, *rows.shape[1:])
        distance //= 2
    return parts.reshape(per_shard, -1, width)


def plan_kernel(mp_count, per_shard, lists, offsets, plan):
    column = lax.axis_index("mp")
    start = offsets[column]
    for j in range(mp_count):
        plan[j] = 0

    def note(p, carry):
        plan[lists[p] // per_shard] = p - start
        return carry

    lax.fori_loop(start, offsets[column + 1], note, 0)

    def owner(p, carry):
        block = lists[p]

        @pl.when(block // per_shard == column)
        def _():
            plan[mp_count + block % per_shard] = lax.fori_loop(
                0, mp_count, lambda c, total: total + (offsets[c + 1] <= p).astype(jnp.int32), 0
            )

        return carry

    lax.fori_loop(0, lists.shape[0], owner, 0)


def right_kernel(mp_count, plan, slots, *outs):
    column = lax.axis_index("mp")
    for d in range(mp_count):
        outs[d][...] = slots[plan[column ^ d]]


def left_kernel(mp_count, plan, slots, half_sq, out):
    rows = slots.shape[1]
    lanes = out.shape[2]
    total = jnp.sum(half_sq[...], axis=0, keepdims=True)
    first = total.astype(jnp.bfloat16).astype(jnp.float32)
    second = (total - first).astype(jnp.bfloat16).astype(jnp.float32)
    third = total - first - second
    row = lax.broadcasted_iota(jnp.int32, (16, lanes), 0)
    parts = jnp.where(row == 0, first, jnp.where(row == 1, second, jnp.where(row == 2, third, 0.0)))
    parts = parts.astype(jnp.bfloat16)
    for j in range(mp_count):
        slot = plan[j]
        for c in range(slots.shape[2] // lanes):
            out[j, c * rows : (c + 1) * rows, :] = slots[slot, :, c * lanes : (c + 1) * lanes]
        out[j, out.shape[1] - 16 :, :] = parts


def pick_kernel(mp_count, per_shard, plan, *refs):
    arrived, out = refs[:mp_count], refs[-1]
    shard = lax.axis_index("mp")
    for r in range(per_shard):
        source = plan[mp_count + r] ^ shard
        for d in range(mp_count):

            @pl.when(source == d)
            def _(d=d, r=r):
                out[r] = arrived[d][...]


def precond_kernel(mp_count, per_shard, plan, right_prod, half_sq, arrived, precond, stats, left):
    rows, lanes = left.shape[0], arrived.shape[2]
    stats[...] = jnp.zeros_like(stats)
    stats[per_shard : 2 * per_shard, :] = half_sq[...]
    parts = jnp.sum(arrived[:, arrived.shape[1] - 16 :, :].astype(jnp.float32), axis=0)
    stats[2 * per_shard : 2 * per_shard + 1, :] = jnp.sum(parts, axis=0, keepdims=True)
    for r in range(per_shard):
        source = plan[mp_count + r]
        for c in range(left.shape[1] // lanes):
            left[:, c * lanes : (c + 1) * lanes] = arrived[source, c * rows : (c + 1) * rows, :]
        product = jnp.dot(left[...], right_prod[r], preferred_element_type=jnp.float32)
        precond[r] = product
        total = jnp.sum(jnp.sum(product * product, axis=1, keepdims=True), axis=0, keepdims=True)
        stats[r : r + 1, :] = jnp.broadcast_to(total, (1, lanes))


def finish_kernel(area, cells, precond, *refs):
    parts, update = refs[:-1], refs[-1]
    per_shard = update.shape[0]
    total = parts[0][...]
    for part in parts[1:]:
        total += part[...]
    precond_sq, block_sq = total[:per_shard], total[per_shard : 2 * per_shard]
    square_total = total[2 * per_shard : 2 * per_shard + 1]
    graft = jnp.sqrt(block_sq / area + epsilon) / jnp.sqrt(precond_sq / area + epsilon)
    scale = max_rms / jnp.sqrt(square_total / cells + epsilon) * graft
    for r in range(per_shard):
        update[r] = (scale[r : r + 1, :1] * precond[r]).astype(update.dtype)


def shards(grad_partials, owner_lists, owner_offsets, left_roots, right_roots):
    dp_count = lax.axis_size("dp")
    mp_count = lax.axis_size("mp")
    dp_index = lax.axis_index("dp")
    partial_blocks = grad_partials[0]
    per_shard = partial_blocks.shape[0]
    width = partial_blocks.shape[2]
    rows = width // dp_count
    area = width * width
    cells = owner_lists.shape[0] * area
    piece = jax.ShapeDtypeStruct((rows, width), jnp.bfloat16)
    lanes = 128

    params = pltpu.CompilerParams(vmem_limit_bytes=16 * 2**20)

    def over_dp(factor):
        return lax.all_to_all(
            factor[0, 0].reshape(dp_count, rows, width), "dp", split_axis=0, concat_axis=0, tiled=True
        )

    plan = pl.pallas_call(
        functools.partial(plan_kernel, mp_count, per_shard),
        out_shape=jax.ShapeDtypeStruct((mp_count + per_shard,), jnp.int32),
        in_specs=[SMEM, SMEM],
        out_specs=SMEM,
        compiler_params=params,
    )(owner_lists, owner_offsets)
    right_slots = over_dp(right_roots)
    total = core_sum(partial_blocks, dp_index)
    right_slots, total, plan = lax.optimization_barrier((right_slots, total, plan))
    outgoing = pl.pallas_call(
        functools.partial(right_kernel, mp_count),
        out_shape=[piece] * mp_count,
        in_specs=[SMEM, VMEM],
        out_specs=[VMEM] * mp_count,
        compiler_params=params,
    )(plan, right_slots)
    left_slots = over_dp(left_roots)
    right_arrived = [outgoing[0]] + [swap(outgoing[d], "mp", d) for d in range(1, mp_count)]
    total = chip_sum(total, dp_count)
    total_f = total.astype(jnp.float32)
    half_sq = jnp.broadcast_to(
        (jnp.sum(total_f * total_f, axis=(1, 2)) * (2 / dp_count)).reshape(per_shard, 1),
        (per_shard, lanes),
    )
    left_outgoing = pl.pallas_call(
        functools.partial(left_kernel, mp_count),
        out_shape=jax.ShapeDtypeStruct((mp_count, rows * width // lanes + 16, lanes), jnp.bfloat16),
        in_specs=[SMEM, VMEM, VMEM],
        out_specs=VMEM,
        compiler_params=params,
    )(plan, left_slots, half_sq)
    left_arrived = lax.all_to_all(left_outgoing, "mp", split_axis=0, concat_axis=0, tiled=True)
    right_rows = pl.pallas_call(
        functools.partial(pick_kernel, mp_count, per_shard),
        out_shape=jax.ShapeDtypeStruct((per_shard, rows, width), jnp.bfloat16),
        in_specs=[SMEM] + [VMEM] * mp_count + [ANY],
        out_specs=VMEM,
        compiler_params=params,
    )(plan, *right_arrived, left_outgoing)
    right = gather_rows(right_rows, dp_count, dp_index)

    grad = both_halves(total, dp_index)
    right_prod = jnp.einsum(
        "bij,bjk->bik", grad, right, preferred_element_type=jnp.float32
    ).astype(jnp.bfloat16)
    precond, stats = pl.pallas_call(
        functools.partial(precond_kernel, mp_count, per_shard),
        out_shape=[
            jax.ShapeDtypeStruct((per_shard, rows, width), jnp.float32),
            jax.ShapeDtypeStruct((pl.cdiv(2 * per_shard + 1, 8) * 8, lanes), jnp.float32),
        ],
        in_specs=[SMEM, VMEM, VMEM, VMEM],
        out_specs=[VMEM, VMEM],
        scratch_shapes=[pltpu.VMEM((rows, width), jnp.bfloat16)],
        compiler_params=params,
    )(plan, right_prod, half_sq, left_arrived)
    parts = [stats] + [swap(stats, "dp", d) for d in range(1, dp_count)]
    return pl.pallas_call(
        functools.partial(finish_kernel, area, cells),
        out_shape=jax.ShapeDtypeStruct((per_shard, rows, width), jnp.bfloat16),
        in_specs=[VMEM] * (1 + dp_count),
        out_specs=VMEM,
        compiler_params=params,
    )(precond, *parts)


def solution(mesh):
    return jax.shard_map(
        shards,
        mesh=mesh,
        in_specs=(
            P("dp", "mp", None, None),
            P(),
            P(),
            P("mp", "dp", None, None),
            P("mp", "dp", None, None),
        ),
        out_specs=P("mp", "dp", None),
        check_vma=False,
    )
```

```python
import functools

import jax
import jax.numpy as jnp
from jax import lax
from jax.experimental import pallas as pl
from jax.experimental.pallas import tpu as pltpu
from jax.sharding import PartitionSpec as P

epsilon = 1e-06
max_rms = 1.0

SMEM = pl.BlockSpec(memory_space=pltpu.SMEM)
VMEM = pl.BlockSpec(memory_space=pltpu.VMEM)
ANY = pl.BlockSpec(memory_space=pl.ANY)


def swap(value, axis, distance):
    count = lax.axis_size(axis)
    return lax.ppermute(value, axis, [(i, i ^ distance) for i in range(count)])


def add_rounded(a, b):
    return (a.astype(jnp.float32) + b.astype(jnp.float32)).astype(jnp.bfloat16)


def core_sum(partial_blocks, dp_index):
    half = partial_blocks.shape[1] // 2
    core = dp_index % 2
    kept = lax.dynamic_slice_in_dim(partial_blocks, core * half, half, axis=1)
    given = lax.dynamic_slice_in_dim(partial_blocks, (1 - core) * half, half, axis=1)
    return add_rounded(kept, swap(given, "dp", 1))


def chip_sum(total, dp_count):
    distance = 2
    while distance < dp_count:
        total = add_rounded(total, swap(total, "dp", distance))
        distance *= 2
    return total


def both_halves(total, dp_index):
    core = dp_index % 2
    other = swap(total, "dp", 1)
    low = jnp.where(core == 0, total, other)
    high = jnp.where(core == 0, other, total)
    return jnp.concatenate([low, high], axis=1)


def gather_rows(rows, dp_count, dp_index):
    per_shard, _, width = rows.shape
    parts = rows[:, None]
    distance = dp_count // 2
    while distance >= 1:
        other = swap(parts, "dp", distance)
        bit = (dp_index // distance) % 2
        low = jnp.where(bit == 0, parts, other)
        high = jnp.where(bit == 0, other, parts)
        parts = jnp.stack([low, high], axis=2)
        parts = parts.reshape(per_shard, -1, *rows.shape[1:])
        distance //= 2
    return parts.reshape(per_shard, -1, width)


def plan_kernel(mp_count, per_shard, lists, offsets, plan):
    column = lax.axis_index("mp")
    start = offsets[column]
    for j in range(mp_count):
        plan[j] = 0

    def note(p, carry):
        plan[lists[p] // per_shard] = p - start
        return carry

    lax.fori_loop(start, offsets[column + 1], note, 0)

    def owner(p, carry):
        block = lists[p]

        @pl.when(block // per_shard == column)
        def _():
            plan[mp_count + block % per_shard] = lax.fori_loop(
                0, mp_count, lambda c, total: total + (offsets[c + 1] <= p).astype(jnp.int32), 0
            )

        return carry

    lax.fori_loop(0, lists.shape[0], owner, 0)


def right_kernel(mp_count, plan, slots, *outs):
    column = lax.axis_index("mp")
    for d in range(mp_count):
        outs[d][...] = slots[plan[column ^ d]]


def left_kernel(mp_count, plan, slots, half_sq, out):
    rows = slots.shape[1]
    lanes = out.shape[2]
    total = jnp.sum(half_sq[...], axis=0, keepdims=True)
    first = total.astype(jnp.bfloat16).astype(jnp.float32)
    second = (total - first).astype(jnp.bfloat16).astype(jnp.float32)
    third = total - first - second
    row = lax.broadcasted_iota(jnp.int32, (16, lanes), 0)
    parts = jnp.where(row == 0, first, jnp.where(row == 1, second, jnp.where(row == 2, third, 0.0)))
    parts = parts.astype(jnp.bfloat16)
    for j in range(mp_count):
        slot = plan[j]
        for c in range(slots.shape[2] // lanes):
            out[j, c * rows : (c + 1) * rows, :] = slots[slot, :, c * lanes : (c + 1) * lanes]
        out[j, out.shape[1] - 16 :, :] = parts


def pick_kernel(mp_count, per_shard, order, plan, *refs):
    arrived, out = dict(zip(order, refs)), refs[-1]
    shard = lax.axis_index("mp")
    for r in range(per_shard):
        source = plan[mp_count + r] ^ shard
        for d in range(mp_count):

            @pl.when(source == d)
            def _(d=d, r=r):
                out[r] = arrived[d][...]


def precond_kernel(mp_count, per_shard, plan, right_prod, half_sq, arrived, precond, stats, left):
    rows, lanes = left.shape[0], arrived.shape[2]
    stats[...] = jnp.zeros_like(stats)
    stats[per_shard : 2 * per_shard, :] = half_sq[...]
    parts = jnp.sum(arrived[:, arrived.shape[1] - 16 :, :].astype(jnp.float32), axis=0)
    stats[2 * per_shard : 2 * per_shard + 1, :] = jnp.sum(parts, axis=0, keepdims=True)
    for r in range(per_shard):
        source = plan[mp_count + r]
        for c in range(left.shape[1] // lanes):
            left[:, c * lanes : (c + 1) * lanes] = arrived[source, c * rows : (c + 1) * rows, :]
        product = jnp.dot(left[...], right_prod[r], preferred_element_type=jnp.float32)
        precond[r] = product
        total = jnp.sum(jnp.sum(product * product, axis=1, keepdims=True), axis=0, keepdims=True)
        stats[r : r + 1, :] = jnp.broadcast_to(total, (1, lanes))


def finish_kernel(area, cells, precond, *refs):
    parts, update = refs[:-1], refs[-1]
    per_shard = update.shape[0]
    total = parts[0][...]
    for part in parts[1:]:
        total += part[...]
    precond_sq, block_sq = total[:per_shard], total[per_shard : 2 * per_shard]
    square_total = total[2 * per_shard : 2 * per_shard + 1]
    graft = jnp.sqrt(block_sq / area + epsilon) / jnp.sqrt(precond_sq / area + epsilon)
    scale = max_rms / jnp.sqrt(square_total / cells + epsilon) * graft
    for r in range(per_shard):
        update[r] = (scale[r : r + 1, :1] * precond[r]).astype(update.dtype)


def shards(grad_partials, owner_lists, owner_offsets, left_roots, right_roots):
    dp_count = lax.axis_size("dp")
    mp_count = lax.axis_size("mp")
    dp_index = lax.axis_index("dp")
    partial_blocks = grad_partials[0]
    per_shard = partial_blocks.shape[0]
    width = partial_blocks.shape[2]
    rows = width // dp_count
    area = width * width
    cells = owner_lists.shape[0] * area
    piece = jax.ShapeDtypeStruct((rows, width), jnp.bfloat16)
    lanes = 128

    params = pltpu.CompilerParams(vmem_limit_bytes=16 * 2**20)

    def over_dp(factor):
        return lax.all_to_all(
            factor[0, 0].reshape(dp_count, rows, width), "dp", split_axis=0, concat_axis=0, tiled=True
        )

    plan = pl.pallas_call(
        functools.partial(plan_kernel, mp_count, per_shard),
        out_shape=jax.ShapeDtypeStruct((mp_count + per_shard,), jnp.int32),
        in_specs=[SMEM, SMEM],
        out_specs=SMEM,
        compiler_params=params,
    )(owner_lists, owner_offsets)
    right_slots = over_dp(right_roots)
    total = core_sum(partial_blocks, dp_index)
    right_slots, total, plan = lax.optimization_barrier((right_slots, total, plan))
    outgoing = pl.pallas_call(
        functools.partial(right_kernel, mp_count),
        out_shape=[piece] * mp_count,
        in_specs=[SMEM, VMEM],
        out_specs=[VMEM] * mp_count,
        compiler_params=params,
    )(plan, right_slots)
    left_slots = over_dp(left_roots)
    far = mp_count // 2
    order = [1, far, *range(2, far), *range(far + 1, mp_count)]
    right_arrived = [outgoing[0]] + [swap(outgoing[d], "mp", d) for d in order]
    total = chip_sum(total, dp_count)
    total_f = total.astype(jnp.float32)
    half_sq = jnp.broadcast_to(
        (jnp.sum(total_f * total_f, axis=(1, 2)) * (2 / dp_count)).reshape(per_shard, 1),
        (per_shard, lanes),
    )
    left_outgoing = pl.pallas_call(
        functools.partial(left_kernel, mp_count),
        out_shape=jax.ShapeDtypeStruct((mp_count, rows * width // lanes + 16, lanes), jnp.bfloat16),
        in_specs=[SMEM, VMEM, VMEM],
        out_specs=VMEM,
        compiler_params=params,
    )(plan, left_slots, half_sq)
    left_arrived = lax.all_to_all(left_outgoing, "mp", split_axis=0, concat_axis=0, tiled=True)
    right_rows = pl.pallas_call(
        functools.partial(pick_kernel, mp_count, per_shard, [0] + order),
        out_shape=jax.ShapeDtypeStruct((per_shard, rows, width), jnp.bfloat16),
        in_specs=[SMEM] + [VMEM] * mp_count + [ANY],
        out_specs=VMEM,
        compiler_params=params,
    )(plan, *right_arrived, left_outgoing)
    right = gather_rows(right_rows, dp_count, dp_index)

    grad = both_halves(total, dp_index)
    right_prod = jnp.einsum(
        "bij,bjk->bik", grad, right, preferred_element_type=jnp.float32
    ).astype(jnp.bfloat16)
    precond, stats = pl.pallas_call(
        functools.partial(precond_kernel, mp_count, per_shard),
        out_shape=[
            jax.ShapeDtypeStruct((per_shard, rows, width), jnp.float32),
            jax.ShapeDtypeStruct((pl.cdiv(2 * per_shard + 1, 8) * 8, lanes), jnp.float32),
        ],
        in_specs=[SMEM, VMEM, VMEM, VMEM],
        out_specs=[VMEM, VMEM],
        scratch_shapes=[pltpu.VMEM((rows, width), jnp.bfloat16)],
        compiler_params=params,
    )(plan, right_prod, half_sq, left_arrived)
    parts = [stats] + [swap(stats, "dp", d) for d in range(1, dp_count)]
    return pl.pallas_call(
        functools.partial(finish_kernel, area, cells),
        out_shape=jax.ShapeDtypeStruct((per_shard, rows, width), jnp.bfloat16),
        in_specs=[VMEM] * (1 + dp_count),
        out_specs=VMEM,
        compiler_params=params,
    )(precond, *parts)


def solution(mesh):
    return jax.shard_map(
        shards,
        mesh=mesh,
        in_specs=(
            P("dp", "mp", None, None),
            P(),
            P(),
            P("mp", "dp", None, None),
            P("mp", "dp", None, None),
        ),
        out_specs=P("mp", "dp", None),
        check_vma=False,
    )
```

```python
import functools

import jax
import jax.numpy as jnp
from jax import lax
from jax.experimental import pallas as pl
from jax.experimental.pallas import tpu as pltpu
from jax.sharding import PartitionSpec as P

epsilon = 1e-06
max_rms = 1.0

SMEM = pl.BlockSpec(memory_space=pltpu.SMEM)
VMEM = pl.BlockSpec(memory_space=pltpu.VMEM)
ANY = pl.BlockSpec(memory_space=pl.ANY)


def swap(value, axis, distance):
    count = lax.axis_size(axis)
    return lax.ppermute(value, axis, [(i, i ^ distance) for i in range(count)])


def add_rounded(a, b):
    return (a.astype(jnp.float32) + b.astype(jnp.float32)).astype(jnp.bfloat16)


def core_sum(partial_blocks, dp_index):
    half = partial_blocks.shape[1] // 2
    core = dp_index % 2
    kept = lax.dynamic_slice_in_dim(partial_blocks, core * half, half, axis=1)
    given = lax.dynamic_slice_in_dim(partial_blocks, (1 - core) * half, half, axis=1)
    return add_rounded(kept, swap(given, "dp", 1))


def chip_sum(total, dp_count, dp_index):
    distance = 2
    while distance < dp_count:
        part = total.shape[1] // 2
        bit = (dp_index // distance) % 2
        kept = lax.dynamic_slice_in_dim(total, bit * part, part, axis=1)
        given = lax.dynamic_slice_in_dim(total, (1 - bit) * part, part, axis=1)
        total = add_rounded(kept, swap(given, "dp", distance))
        distance *= 2
    return total


def whole_rows(total, dp_count, dp_index):
    part = total.shape[1]
    whole = jnp.zeros((total.shape[0], part * dp_count, total.shape[2]), total.dtype)
    for d in range(dp_count):
        piece = swap(total, "dp", d) if d else total
        holder, place, distance = dp_index ^ d, 0, 1
        while distance < dp_count:
            place = 2 * place + (holder // distance) % 2
            distance *= 2
        whole = lax.dynamic_update_slice_in_dim(whole, piece, place * part, axis=1)
    return whole


def gather_rows(rows, dp_count, dp_index):
    per_shard, _, width = rows.shape
    parts = rows[:, None]
    distance = dp_count // 2
    while distance >= 1:
        other = swap(parts, "dp", distance)
        bit = (dp_index // distance) % 2
        low = jnp.where(bit == 0, parts, other)
        high = jnp.where(bit == 0, other, parts)
        parts = jnp.stack([low, high], axis=2)
        parts = parts.reshape(per_shard, -1, *rows.shape[1:])
        distance //= 2
    return parts.reshape(per_shard, -1, width)


def plan_kernel(mp_count, per_shard, lists, offsets, plan):
    column = lax.axis_index("mp")
    start = offsets[column]
    for j in range(mp_count):
        plan[j] = 0

    def note(p, carry):
        plan[lists[p] // per_shard] = p - start
        return carry

    lax.fori_loop(start, offsets[column + 1], note, 0)

    def owner(p, carry):
        block = lists[p]

        @pl.when(block // per_shard == column)
        def _():
            plan[mp_count + block % per_shard] = lax.fori_loop(
                0, mp_count, lambda c, total: total + (offsets[c + 1] <= p).astype(jnp.int32), 0
            )

        return carry

    lax.fori_loop(0, lists.shape[0], owner, 0)


def right_kernel(mp_count, plan, slots, *outs):
    column = lax.axis_index("mp")
    for d in range(mp_count):
        outs[d][...] = slots[plan[column ^ d]]


def left_kernel(mp_count, plan, slots, half_sq, out):
    rows = slots.shape[1]
    lanes = out.shape[2]
    total = jnp.sum(half_sq[...], axis=0, keepdims=True)
    first = total.astype(jnp.bfloat16).astype(jnp.float32)
    second = (total - first).astype(jnp.bfloat16).astype(jnp.float32)
    third = total - first - second
    row = lax.broadcasted_iota(jnp.int32, (16, lanes), 0)
    parts = jnp.where(row == 0, first, jnp.where(row == 1, second, jnp.where(row == 2, third, 0.0)))
    parts = parts.astype(jnp.bfloat16)
    for j in range(mp_count):
        slot = plan[j]
        for c in range(slots.shape[2] // lanes):
            out[j, c * rows : (c + 1) * rows, :] = slots[slot, :, c * lanes : (c + 1) * lanes]
        out[j, out.shape[1] - 16 :, :] = parts


def pick_kernel(mp_count, per_shard, order, plan, *refs):
    arrived, out = dict(zip(order, refs)), refs[-1]
    shard = lax.axis_index("mp")
    for r in range(per_shard):
        source = plan[mp_count + r] ^ shard
        for d in range(mp_count):

            @pl.when(source == d)
            def _(d=d, r=r):
                out[r] = arrived[d][...]


def precond_kernel(mp_count, per_shard, plan, right_prod, half_sq, arrived, precond, stats, left):
    rows, lanes = left.shape[0], arrived.shape[2]
    stats[...] = jnp.zeros_like(stats)
    stats[per_shard : 2 * per_shard, :] = half_sq[...]
    parts = jnp.sum(arrived[:, arrived.shape[1] - 16 :, :].astype(jnp.float32), axis=0)
    stats[2 * per_shard : 2 * per_shard + 1, :] = jnp.sum(parts, axis=0, keepdims=True)
    for r in range(per_shard):
        source = plan[mp_count + r]
        for c in range(left.shape[1] // lanes):
            left[:, c * lanes : (c + 1) * lanes] = arrived[source, c * rows : (c + 1) * rows, :]
        product = jnp.dot(left[...], right_prod[r], preferred_element_type=jnp.float32)
        precond[r] = product
        total = jnp.sum(jnp.sum(product * product, axis=1, keepdims=True), axis=0, keepdims=True)
        stats[r : r + 1, :] = jnp.broadcast_to(total, (1, lanes))


def finish_kernel(area, cells, precond, *refs):
    parts, update = refs[:-1], refs[-1]
    per_shard = update.shape[0]
    total = parts[0][...]
    for part in parts[1:]:
        total += part[...]
    precond_sq, block_sq = total[:per_shard], total[per_shard : 2 * per_shard]
    square_total = total[2 * per_shard : 2 * per_shard + 1]
    graft = jnp.sqrt(block_sq / area + epsilon) / jnp.sqrt(precond_sq / area + epsilon)
    scale = max_rms / jnp.sqrt(square_total / cells + epsilon) * graft
    for r in range(per_shard):
        update[r] = (scale[r : r + 1, :1] * precond[r]).astype(update.dtype)


def shards(grad_partials, owner_lists, owner_offsets, left_roots, right_roots):
    dp_count = lax.axis_size("dp")
    mp_count = lax.axis_size("mp")
    dp_index = lax.axis_index("dp")
    partial_blocks = grad_partials[0]
    per_shard = partial_blocks.shape[0]
    width = partial_blocks.shape[2]
    rows = width // dp_count
    area = width * width
    cells = owner_lists.shape[0] * area
    piece = jax.ShapeDtypeStruct((rows, width), jnp.bfloat16)
    lanes = 128

    params = pltpu.CompilerParams(vmem_limit_bytes=16 * 2**20)

    def over_dp(factor):
        return lax.all_to_all(
            factor[0, 0].reshape(dp_count, rows, width), "dp", split_axis=0, concat_axis=0, tiled=True
        )

    plan = pl.pallas_call(
        functools.partial(plan_kernel, mp_count, per_shard),
        out_shape=jax.ShapeDtypeStruct((mp_count + per_shard,), jnp.int32),
        in_specs=[SMEM, SMEM],
        out_specs=SMEM,
        compiler_params=params,
    )(owner_lists, owner_offsets)
    right_slots = over_dp(right_roots)
    total = core_sum(partial_blocks, dp_index)
    right_slots, total, plan = lax.optimization_barrier((right_slots, total, plan))
    outgoing = pl.pallas_call(
        functools.partial(right_kernel, mp_count),
        out_shape=[piece] * mp_count,
        in_specs=[SMEM, VMEM],
        out_specs=[VMEM] * mp_count,
        compiler_params=params,
    )(plan, right_slots)
    left_slots = over_dp(left_roots)
    far = mp_count // 2
    order = [1, far, *range(2, far), *range(far + 1, mp_count)]
    right_arrived = [outgoing[0]] + [swap(outgoing[d], "mp", d) for d in order]
    total = chip_sum(total, dp_count, dp_index)
    total_f = total.astype(jnp.float32)
    half_sq = jnp.broadcast_to(
        jnp.sum(total_f * total_f, axis=(1, 2)).reshape(per_shard, 1),
        (per_shard, lanes),
    )
    left_outgoing = pl.pallas_call(
        functools.partial(left_kernel, mp_count),
        out_shape=jax.ShapeDtypeStruct((mp_count, rows * width // lanes + 16, lanes), jnp.bfloat16),
        in_specs=[SMEM, VMEM, VMEM],
        out_specs=VMEM,
        compiler_params=params,
    )(plan, left_slots, half_sq)
    left_arrived = lax.all_to_all(left_outgoing, "mp", split_axis=0, concat_axis=0, tiled=True)
    right_rows = pl.pallas_call(
        functools.partial(pick_kernel, mp_count, per_shard, [0] + order),
        out_shape=jax.ShapeDtypeStruct((per_shard, rows, width), jnp.bfloat16),
        in_specs=[SMEM] + [VMEM] * mp_count + [ANY],
        out_specs=VMEM,
        compiler_params=params,
    )(plan, *right_arrived, left_outgoing)
    right = gather_rows(right_rows, dp_count, dp_index)

    grad = whole_rows(total, dp_count, dp_index)
    right_prod = jnp.einsum(
        "bij,bjk->bik", grad, right, preferred_element_type=jnp.float32
    ).astype(jnp.bfloat16)
    precond, stats = pl.pallas_call(
        functools.partial(precond_kernel, mp_count, per_shard),
        out_shape=[
            jax.ShapeDtypeStruct((per_shard, rows, width), jnp.float32),
            jax.ShapeDtypeStruct((pl.cdiv(2 * per_shard + 1, 8) * 8, lanes), jnp.float32),
        ],
        in_specs=[SMEM, VMEM, VMEM, VMEM],
        out_specs=[VMEM, VMEM],
        scratch_shapes=[pltpu.VMEM((rows, width), jnp.bfloat16)],
        compiler_params=params,
    )(plan, right_prod, half_sq, left_arrived)
    parts = [stats] + [swap(stats, "dp", d) for d in range(1, dp_count)]
    return pl.pallas_call(
        functools.partial(finish_kernel, area, cells),
        out_shape=jax.ShapeDtypeStruct((per_shard, rows, width), jnp.bfloat16),
        in_specs=[VMEM] * (1 + dp_count),
        out_specs=VMEM,
        compiler_params=params,
    )(precond, *parts)


def solution(mesh):
    return jax.shard_map(
        shards,
        mesh=mesh,
        in_specs=(
            P("dp", "mp", None, None),
            P(),
            P(),
            P("mp", "dp", None, None),
            P("mp", "dp", None, None),
        ),
        out_specs=P("mp", "dp", None),
        check_vma=False,
    )
```

```python
import functools

import jax
import jax.numpy as jnp
from jax import lax
from jax.experimental import pallas as pl
from jax.experimental.pallas import tpu as pltpu
from jax.sharding import PartitionSpec as P

epsilon = 1e-06
max_rms = 1.0

SMEM = pl.BlockSpec(memory_space=pltpu.SMEM)
VMEM = pl.BlockSpec(memory_space=pltpu.VMEM)
ANY = pl.BlockSpec(memory_space=pl.ANY)


def swap(value, axis, distance):
    count = lax.axis_size(axis)
    return lax.ppermute(value, axis, [(i, i ^ distance) for i in range(count)])


def add_rounded(a, b):
    return (a.astype(jnp.float32) + b.astype(jnp.float32)).astype(jnp.bfloat16)


def core_sum(partial_blocks, dp_index):
    half = partial_blocks.shape[1] // 2
    core = dp_index % 2
    kept = lax.dynamic_slice_in_dim(partial_blocks, core * half, half, axis=1)
    given = lax.dynamic_slice_in_dim(partial_blocks, (1 - core) * half, half, axis=1)
    return add_rounded(kept, swap(given, "dp", 1))


def chip_sum(total, dp_count, dp_index):
    distance = 2
    while distance < dp_count:
        part = total.shape[1] // 2
        bit = (dp_index // distance) % 2
        kept = lax.dynamic_slice_in_dim(total, bit * part, part, axis=1)
        given = lax.dynamic_slice_in_dim(total, (1 - bit) * part, part, axis=1)
        total = add_rounded(kept, swap(given, "dp", distance))
        distance *= 2
    return total


def whole_rows(total, dp_count, dp_index):
    part = total.shape[1]
    pieces, distance = {0: total}, dp_count // 2
    while distance >= 1:
        pieces |= {d ^ distance: swap(piece, "dp", distance) for d, piece in pieces.items()}
        distance //= 2
    whole = jnp.zeros((total.shape[0], part * dp_count, total.shape[2]), total.dtype)
    for d, piece in pieces.items():
        holder, place, distance = dp_index ^ d, 0, 1
        while distance < dp_count:
            place = 2 * place + (holder // distance) % 2
            distance *= 2
        whole = lax.dynamic_update_slice_in_dim(whole, piece, place * part, axis=1)
    return whole


def gather_rows(rows, dp_count, dp_index):
    per_shard, _, width = rows.shape
    parts = rows[:, None]
    distance = dp_count // 2
    while distance >= 1:
        other = swap(parts, "dp", distance)
        bit = (dp_index // distance) % 2
        low = jnp.where(bit == 0, parts, other)
        high = jnp.where(bit == 0, other, parts)
        parts = jnp.stack([low, high], axis=2)
        parts = parts.reshape(per_shard, -1, *rows.shape[1:])
        distance //= 2
    return parts.reshape(per_shard, -1, width)


def plan_kernel(mp_count, per_shard, lists, offsets, plan):
    column = lax.axis_index("mp")
    start = offsets[column]
    for j in range(mp_count):
        plan[j] = 0

    def note(p, carry):
        plan[lists[p] // per_shard] = p - start
        return carry

    lax.fori_loop(start, offsets[column + 1], note, 0)

    def owner(p, carry):
        block = lists[p]

        @pl.when(block // per_shard == column)
        def _():
            plan[mp_count + block % per_shard] = lax.fori_loop(
                0, mp_count, lambda c, total: total + (offsets[c + 1] <= p).astype(jnp.int32), 0
            )

        return carry

    lax.fori_loop(0, lists.shape[0], owner, 0)


def right_kernel(mp_count, plan, slots, *outs):
    column = lax.axis_index("mp")
    for d in range(mp_count):
        outs[d][...] = slots[plan[column ^ d]]


def left_kernel(mp_count, plan, slots, half_sq, out):
    rows = slots.shape[1]
    lanes = out.shape[2]
    total = jnp.sum(half_sq[...], axis=0, keepdims=True)
    first = total.astype(jnp.bfloat16).astype(jnp.float32)
    second = (total - first).astype(jnp.bfloat16).astype(jnp.float32)
    third = total - first - second
    row = lax.broadcasted_iota(jnp.int32, (16, lanes), 0)
    parts = jnp.where(row == 0, first, jnp.where(row == 1, second, jnp.where(row == 2, third, 0.0)))
    parts = parts.astype(jnp.bfloat16)
    for j in range(mp_count):
        slot = plan[j]
        for c in range(slots.shape[2] // lanes):
            out[j, c * rows : (c + 1) * rows, :] = slots[slot, :, c * lanes : (c + 1) * lanes]
        out[j, out.shape[1] - 16 :, :] = parts


def pick_kernel(mp_count, per_shard, order, plan, *refs):
    arrived, out = dict(zip(order, refs)), refs[-1]
    shard = lax.axis_index("mp")
    for r in range(per_shard):
        source = plan[mp_count + r] ^ shard
        for d in range(mp_count):

            @pl.when(source == d)
            def _(d=d, r=r):
                out[r] = arrived[d][...]


def precond_kernel(mp_count, per_shard, plan, right_prod, half_sq, arrived, precond, stats, left):
    rows, lanes = left.shape[0], arrived.shape[2]
    stats[...] = jnp.zeros_like(stats)
    stats[per_shard : 2 * per_shard, :] = half_sq[...]
    parts = jnp.sum(arrived[:, arrived.shape[1] - 16 :, :].astype(jnp.float32), axis=0)
    stats[2 * per_shard : 2 * per_shard + 1, :] = jnp.sum(parts, axis=0, keepdims=True)
    for r in range(per_shard):
        source = plan[mp_count + r]
        for c in range(left.shape[1] // lanes):
            left[:, c * lanes : (c + 1) * lanes] = arrived[source, c * rows : (c + 1) * rows, :]
        product = jnp.dot(left[...], right_prod[r], preferred_element_type=jnp.float32)
        precond[r] = product
        total = jnp.sum(jnp.sum(product * product, axis=1, keepdims=True), axis=0, keepdims=True)
        stats[r : r + 1, :] = jnp.broadcast_to(total, (1, lanes))


def finish_kernel(area, cells, precond, *refs):
    parts, update = refs[:-1], refs[-1]
    per_shard = update.shape[0]
    total = parts[0][...]
    for part in parts[1:]:
        total += part[...]
    precond_sq, block_sq = total[:per_shard], total[per_shard : 2 * per_shard]
    square_total = total[2 * per_shard : 2 * per_shard + 1]
    graft = jnp.sqrt(block_sq / area + epsilon) / jnp.sqrt(precond_sq / area + epsilon)
    scale = max_rms / jnp.sqrt(square_total / cells + epsilon) * graft
    for r in range(per_shard):
        update[r] = (scale[r : r + 1, :1] * precond[r]).astype(update.dtype)


def shards(grad_partials, owner_lists, owner_offsets, left_roots, right_roots):
    dp_count = lax.axis_size("dp")
    mp_count = lax.axis_size("mp")
    dp_index = lax.axis_index("dp")
    partial_blocks = grad_partials[0]
    per_shard = partial_blocks.shape[0]
    width = partial_blocks.shape[2]
    rows = width // dp_count
    area = width * width
    cells = owner_lists.shape[0] * area
    piece = jax.ShapeDtypeStruct((rows, width), jnp.bfloat16)
    lanes = 128

    params = pltpu.CompilerParams(vmem_limit_bytes=16 * 2**20)

    def over_dp(factor):
        return lax.all_to_all(
            factor[0, 0].reshape(dp_count, rows, width), "dp", split_axis=0, concat_axis=0, tiled=True
        )

    plan = pl.pallas_call(
        functools.partial(plan_kernel, mp_count, per_shard),
        out_shape=jax.ShapeDtypeStruct((mp_count + per_shard,), jnp.int32),
        in_specs=[SMEM, SMEM],
        out_specs=SMEM,
        compiler_params=params,
    )(owner_lists, owner_offsets)
    right_slots = over_dp(right_roots)
    total = core_sum(partial_blocks, dp_index)
    right_slots, total, plan = lax.optimization_barrier((right_slots, total, plan))
    outgoing = pl.pallas_call(
        functools.partial(right_kernel, mp_count),
        out_shape=[piece] * mp_count,
        in_specs=[SMEM, VMEM],
        out_specs=[VMEM] * mp_count,
        compiler_params=params,
    )(plan, right_slots)
    left_slots = over_dp(left_roots)
    far = mp_count // 2
    order = [1, far, *range(2, far), *range(far + 1, mp_count)]
    right_arrived = [outgoing[0]] + [swap(outgoing[d], "mp", d) for d in order]
    total = chip_sum(total, dp_count, dp_index)
    total_f = total.astype(jnp.float32)
    half_sq = jnp.broadcast_to(
        jnp.sum(total_f * total_f, axis=(1, 2)).reshape(per_shard, 1),
        (per_shard, lanes),
    )
    left_outgoing = pl.pallas_call(
        functools.partial(left_kernel, mp_count),
        out_shape=jax.ShapeDtypeStruct((mp_count, rows * width // lanes + 16, lanes), jnp.bfloat16),
        in_specs=[SMEM, VMEM, VMEM],
        out_specs=VMEM,
        compiler_params=params,
    )(plan, left_slots, half_sq)
    left_arrived = lax.all_to_all(left_outgoing, "mp", split_axis=0, concat_axis=0, tiled=True)
    right_rows = pl.pallas_call(
        functools.partial(pick_kernel, mp_count, per_shard, [0] + order),
        out_shape=jax.ShapeDtypeStruct((per_shard, rows, width), jnp.bfloat16),
        in_specs=[SMEM] + [VMEM] * mp_count + [ANY],
        out_specs=VMEM,
        compiler_params=params,
    )(plan, *right_arrived, left_outgoing)
    right = gather_rows(right_rows, dp_count, dp_index)

    grad = whole_rows(total, dp_count, dp_index)
    right_prod = jnp.einsum(
        "bij,bjk->bik", grad, right, preferred_element_type=jnp.float32
    ).astype(jnp.bfloat16)
    precond, stats = pl.pallas_call(
        functools.partial(precond_kernel, mp_count, per_shard),
        out_shape=[
            jax.ShapeDtypeStruct((per_shard, rows, width), jnp.float32),
            jax.ShapeDtypeStruct((pl.cdiv(2 * per_shard + 1, 8) * 8, lanes), jnp.float32),
        ],
        in_specs=[SMEM, VMEM, VMEM, VMEM],
        out_specs=[VMEM, VMEM],
        scratch_shapes=[pltpu.VMEM((rows, width), jnp.bfloat16)],
        compiler_params=params,
    )(plan, right_prod, half_sq, left_arrived)
    parts = [stats] + [swap(stats, "dp", d) for d in range(1, dp_count)]
    return pl.pallas_call(
        functools.partial(finish_kernel, area, cells),
        out_shape=jax.ShapeDtypeStruct((per_shard, rows, width), jnp.bfloat16),
        in_specs=[VMEM] * (1 + dp_count),
        out_specs=VMEM,
        compiler_params=params,
    )(precond, *parts)


def solution(mesh):
    return jax.shard_map(
        shards,
        mesh=mesh,
        in_specs=(
            P("dp", "mp", None, None),
            P(),
            P(),
            P("mp", "dp", None, None),
            P("mp", "dp", None, None),
        ),
        out_specs=P("mp", "dp", None),
        check_vma=False,
    )
```

```python
import functools

import jax
import jax.numpy as jnp
from jax import lax
from jax.experimental import pallas as pl
from jax.experimental.pallas import tpu as pltpu
from jax.sharding import PartitionSpec as P

epsilon = 1e-06
max_rms = 1.0

SMEM = pl.BlockSpec(memory_space=pltpu.SMEM)
VMEM = pl.BlockSpec(memory_space=pltpu.VMEM)
ANY = pl.BlockSpec(memory_space=pl.ANY)


def swap(value, axis, distance):
    count = lax.axis_size(axis)
    return lax.ppermute(value, axis, [(i, i ^ distance) for i in range(count)])


def add_rounded(a, b):
    return (a.astype(jnp.float32) + b.astype(jnp.float32)).astype(jnp.bfloat16)


def core_sum(partial_blocks, dp_index):
    half = partial_blocks.shape[1] // 2
    core = dp_index % 2
    kept = lax.dynamic_slice_in_dim(partial_blocks, core * half, half, axis=1)
    given = lax.dynamic_slice_in_dim(partial_blocks, (1 - core) * half, half, axis=1)
    return add_rounded(kept, swap(given, "dp", 1))


def chip_sum(total, dp_count, dp_index):
    distance = 2
    while distance < dp_count:
        part = total.shape[1] // 2
        bit = (dp_index // distance) % 2
        kept = lax.dynamic_slice_in_dim(total, bit * part, part, axis=1)
        given = lax.dynamic_slice_in_dim(total, (1 - bit) * part, part, axis=1)
        total = add_rounded(kept, swap(given, "dp", distance))
        distance *= 2
    return total


def whole_rows(total, dp_count, dp_index):
    part = total.shape[1]
    pieces, distance = {0: total}, dp_count // 2
    while distance >= 1:
        pieces |= {d ^ distance: swap(piece, "dp", distance) for d, piece in pieces.items()}
        distance //= 2
    whole = jnp.zeros((total.shape[0], part * dp_count, total.shape[2]), total.dtype)
    for d, piece in pieces.items():
        holder, place, distance = dp_index ^ d, 0, 1
        while distance < dp_count:
            place = 2 * place + (holder // distance) % 2
            distance *= 2
        whole = lax.dynamic_update_slice_in_dim(whole, piece, place * part, axis=1)
    return whole


def gather_rows(rows, dp_count, dp_index):
    per_shard, _, width = rows.shape
    parts = rows[:, None]
    distance = dp_count // 2
    while distance >= 1:
        other = swap(parts, "dp", distance)
        bit = (dp_index // distance) % 2
        low = jnp.where(bit == 0, parts, other)
        high = jnp.where(bit == 0, other, parts)
        parts = jnp.stack([low, high], axis=2)
        parts = parts.reshape(per_shard, -1, *rows.shape[1:])
        distance //= 2
    return parts.reshape(per_shard, -1, width)


def plan_kernel(mp_count, per_shard, lists, offsets, plan):
    column = lax.axis_index("mp")
    start = offsets[column]
    for j in range(mp_count):
        plan[j] = 0

    def note(p, carry):
        plan[lists[p] // per_shard] = p - start
        return carry

    lax.fori_loop(start, offsets[column + 1], note, 0)

    def owner(p, carry):
        block = lists[p]

        @pl.when(block // per_shard == column)
        def _():
            plan[mp_count + block % per_shard] = lax.fori_loop(
                0, mp_count, lambda c, total: total + (offsets[c + 1] <= p).astype(jnp.int32), 0
            )

        return carry

    lax.fori_loop(0, lists.shape[0], owner, 0)


def right_kernel(mp_count, plan, slots, *outs):
    column = lax.axis_index("mp")
    for d in range(mp_count):
        outs[d][...] = slots[plan[column ^ d]]


def left_kernel(mp_count, plan, slots, half_sq, out):
    rows = slots.shape[1]
    lanes = out.shape[2]
    total = jnp.sum(half_sq[...], axis=0, keepdims=True)
    first = total.astype(jnp.bfloat16).astype(jnp.float32)
    second = (total - first).astype(jnp.bfloat16).astype(jnp.float32)
    third = total - first - second
    row = lax.broadcasted_iota(jnp.int32, (16, lanes), 0)
    parts = jnp.where(row == 0, first, jnp.where(row == 1, second, jnp.where(row == 2, third, 0.0)))
    parts = parts.astype(jnp.bfloat16)
    for j in range(mp_count):
        slot = plan[j]
        for c in range(slots.shape[2] // lanes):
            out[j, c * rows : (c + 1) * rows, :] = slots[slot, :, c * lanes : (c + 1) * lanes]
        out[j, out.shape[1] - 16 :, :] = parts


def pick_kernel(mp_count, per_shard, order, plan, *refs):
    arrived, out = dict(zip(order, refs)), refs[-1]
    shard = lax.axis_index("mp")
    for r in range(per_shard):
        source = plan[mp_count + r] ^ shard
        for d in range(mp_count):

            @pl.when(source == d)
            def _(d=d, r=r):
                out[r] = arrived[d][...]


def precond_kernel(mp_count, per_shard, plan, right_prod, half_sq, arrived, precond, stats, left):
    rows, lanes = left.shape[0], arrived.shape[2]
    stats[...] = jnp.zeros_like(stats)
    stats[per_shard : 2 * per_shard, :] = half_sq[...]
    parts = jnp.sum(arrived[:, arrived.shape[1] - 16 :, :].astype(jnp.float32), axis=0)
    stats[2 * per_shard : 2 * per_shard + 1, :] = jnp.sum(parts, axis=0, keepdims=True)
    for r in range(per_shard):
        source = plan[mp_count + r]
        for c in range(left.shape[1] // lanes):
            left[:, c * lanes : (c + 1) * lanes] = arrived[source, c * rows : (c + 1) * rows, :]
        product = jnp.dot(left[...], right_prod[r], preferred_element_type=jnp.float32)
        precond[r] = product
        total = jnp.sum(jnp.sum(product * product, axis=1, keepdims=True), axis=0, keepdims=True)
        stats[r : r + 1, :] = jnp.broadcast_to(total, (1, lanes))


def finish_kernel(area, cells, precond, *refs):
    parts, update = refs[:-1], refs[-1]
    per_shard = update.shape[0]
    total = parts[0][...]
    for part in parts[1:]:
        total += part[...]
    precond_sq, block_sq = total[:per_shard], total[per_shard : 2 * per_shard]
    square_total = total[2 * per_shard : 2 * per_shard + 1]
    graft = jnp.sqrt(block_sq / area + epsilon) / jnp.sqrt(precond_sq / area + epsilon)
    scale = max_rms / jnp.sqrt(square_total / cells + epsilon) * graft
    for r in range(per_shard):
        update[r] = (scale[r : r + 1, :1] * precond[r]).astype(update.dtype)


def shards(grad_partials, owner_lists, owner_offsets, left_roots, right_roots):
    dp_count = lax.axis_size("dp")
    mp_count = lax.axis_size("mp")
    dp_index = lax.axis_index("dp")
    partial_blocks = grad_partials[0]
    per_shard = partial_blocks.shape[0]
    width = partial_blocks.shape[2]
    rows = width // dp_count
    area = width * width
    cells = owner_lists.shape[0] * area
    piece = jax.ShapeDtypeStruct((rows, width), jnp.bfloat16)
    lanes = 128

    params = pltpu.CompilerParams(vmem_limit_bytes=16 * 2**20)

    def over_dp(factor):
        return lax.all_to_all(
            factor[0, 0].reshape(dp_count, rows, width), "dp", split_axis=0, concat_axis=0, tiled=True
        )

    plan = pl.pallas_call(
        functools.partial(plan_kernel, mp_count, per_shard),
        out_shape=jax.ShapeDtypeStruct((mp_count + per_shard,), jnp.int32),
        in_specs=[SMEM, SMEM],
        out_specs=SMEM,
        compiler_params=params,
    )(owner_lists, owner_offsets)
    right_slots = over_dp(right_roots)
    right_slots, plan, partial_blocks = lax.optimization_barrier((right_slots, plan, partial_blocks))
    total = core_sum(partial_blocks, dp_index)
    outgoing = pl.pallas_call(
        functools.partial(right_kernel, mp_count),
        out_shape=[piece] * mp_count,
        in_specs=[SMEM, VMEM],
        out_specs=[VMEM] * mp_count,
        compiler_params=params,
    )(plan, right_slots)
    left_slots = over_dp(left_roots)
    far = mp_count // 2
    order = [1, far, *range(2, far), *range(far + 1, mp_count)]
    right_arrived = [outgoing[0]] + [swap(outgoing[d], "mp", d) for d in order]
    total = chip_sum(total, dp_count, dp_index)
    total_f = total.astype(jnp.float32)
    half_sq = jnp.broadcast_to(
        jnp.sum(total_f * total_f, axis=(1, 2)).reshape(per_shard, 1),
        (per_shard, lanes),
    )
    left_outgoing = pl.pallas_call(
        functools.partial(left_kernel, mp_count),
        out_shape=jax.ShapeDtypeStruct((mp_count, rows * width // lanes + 16, lanes), jnp.bfloat16),
        in_specs=[SMEM, VMEM, VMEM],
        out_specs=VMEM,
        compiler_params=params,
    )(plan, left_slots, half_sq)
    left_arrived = lax.all_to_all(left_outgoing, "mp", split_axis=0, concat_axis=0, tiled=True)
    right_rows = pl.pallas_call(
        functools.partial(pick_kernel, mp_count, per_shard, [0] + order),
        out_shape=jax.ShapeDtypeStruct((per_shard, rows, width), jnp.bfloat16),
        in_specs=[SMEM] + [VMEM] * mp_count + [ANY],
        out_specs=VMEM,
        compiler_params=params,
    )(plan, *right_arrived, left_outgoing)
    right = gather_rows(right_rows, dp_count, dp_index)

    grad = whole_rows(total, dp_count, dp_index)
    right_prod = jnp.einsum(
        "bij,bjk->bik", grad, right, preferred_element_type=jnp.float32
    ).astype(jnp.bfloat16)
    precond, stats = pl.pallas_call(
        functools.partial(precond_kernel, mp_count, per_shard),
        out_shape=[
            jax.ShapeDtypeStruct((per_shard, rows, width), jnp.float32),
            jax.ShapeDtypeStruct((pl.cdiv(2 * per_shard + 1, 8) * 8, lanes), jnp.float32),
        ],
        in_specs=[SMEM, VMEM, VMEM, VMEM],
        out_specs=[VMEM, VMEM],
        scratch_shapes=[pltpu.VMEM((rows, width), jnp.bfloat16)],
        compiler_params=params,
    )(plan, right_prod, half_sq, left_arrived)
    parts = [stats] + [swap(stats, "dp", d) for d in range(1, dp_count)]
    return pl.pallas_call(
        functools.partial(finish_kernel, area, cells),
        out_shape=jax.ShapeDtypeStruct((per_shard, rows, width), jnp.bfloat16),
        in_specs=[VMEM] * (1 + dp_count),
        out_specs=VMEM,
        compiler_params=params,
    )(precond, *parts)


def solution(mesh):
    return jax.shard_map(
        shards,
        mesh=mesh,
        in_specs=(
            P("dp", "mp", None, None),
            P(),
            P(),
            P("mp", "dp", None, None),
            P("mp", "dp", None, None),
        ),
        out_specs=P("mp", "dp", None),
        check_vma=False,
    )
```

```python
import functools

import jax
import jax.numpy as jnp
from jax import lax
from jax.experimental import pallas as pl
from jax.experimental.pallas import tpu as pltpu
from jax.sharding import PartitionSpec as P

epsilon = 1e-06
max_rms = 1.0

SMEM = pl.BlockSpec(memory_space=pltpu.SMEM)
VMEM = pl.BlockSpec(memory_space=pltpu.VMEM)
ANY = pl.BlockSpec(memory_space=pl.ANY)


def swap(value, axis, distance):
    count = lax.axis_size(axis)
    return lax.ppermute(value, axis, [(i, i ^ distance) for i in range(count)])


def add_rounded(a, b):
    return (a.astype(jnp.float32) + b.astype(jnp.float32)).astype(jnp.bfloat16)


def core_sum(partial_blocks, dp_index):
    half = partial_blocks.shape[1] // 2
    core = dp_index % 2
    other = swap(partial_blocks, "dp", 1)
    kept = lax.dynamic_slice_in_dim(partial_blocks, core * half, half, axis=1)
    taken = lax.dynamic_slice_in_dim(other, core * half, half, axis=1)
    return add_rounded(kept, taken)


def chip_sum(total, dp_count, dp_index):
    distance = 2
    while distance < dp_count:
        part = total.shape[1] // 2
        bit = (dp_index // distance) % 2
        kept = lax.dynamic_slice_in_dim(total, bit * part, part, axis=1)
        given = lax.dynamic_slice_in_dim(total, (1 - bit) * part, part, axis=1)
        total = add_rounded(kept, swap(given, "dp", distance))
        distance *= 2
    return total


def whole_rows(total, dp_count, dp_index):
    part = total.shape[1]
    pieces, distance = {0: total}, dp_count // 2
    while distance >= 1:
        pieces |= {d ^ distance: swap(piece, "dp", distance) for d, piece in pieces.items()}
        distance //= 2
    whole = jnp.zeros((total.shape[0], part * dp_count, total.shape[2]), total.dtype)
    for d, piece in pieces.items():
        holder, place, distance = dp_index ^ d, 0, 1
        while distance < dp_count:
            place = 2 * place + (holder // distance) % 2
            distance *= 2
        whole = lax.dynamic_update_slice_in_dim(whole, piece, place * part, axis=1)
    return whole


def gather_rows(rows, dp_count, dp_index):
    per_shard, _, width = rows.shape
    parts = rows[:, None]
    distance = dp_count // 2
    while distance >= 1:
        other = swap(parts, "dp", distance)
        bit = (dp_index // distance) % 2
        low = jnp.where(bit == 0, parts, other)
        high = jnp.where(bit == 0, other, parts)
        parts = jnp.stack([low, high], axis=2)
        parts = parts.reshape(per_shard, -1, *rows.shape[1:])
        distance //= 2
    return parts.reshape(per_shard, -1, width)


def plan_kernel(mp_count, per_shard, lists, offsets, plan):
    column = lax.axis_index("mp")
    start = offsets[column]
    for j in range(mp_count):
        plan[j] = 0

    def note(p, carry):
        plan[lists[p] // per_shard] = p - start
        return carry

    lax.fori_loop(start, offsets[column + 1], note, 0)

    def owner(p, carry):
        block = lists[p]

        @pl.when(block // per_shard == column)
        def _():
            plan[mp_count + block % per_shard] = lax.fori_loop(
                0, mp_count, lambda c, total: total + (offsets[c + 1] <= p).astype(jnp.int32), 0
            )

        return carry

    lax.fori_loop(0, lists.shape[0], owner, 0)


def right_kernel(mp_count, plan, slots, *outs):
    column = lax.axis_index("mp")
    for d in range(mp_count):
        outs[d][...] = slots[plan[column ^ d]]


def left_kernel(mp_count, plan, slots, half_sq, out):
    rows = slots.shape[1]
    lanes = out.shape[2]
    total = jnp.sum(half_sq[...], axis=0, keepdims=True)
    first = total.astype(jnp.bfloat16).astype(jnp.float32)
    second = (total - first).astype(jnp.bfloat16).astype(jnp.float32)
    third = total - first - second
    row = lax.broadcasted_iota(jnp.int32, (16, lanes), 0)
    parts = jnp.where(row == 0, first, jnp.where(row == 1, second, jnp.where(row == 2, third, 0.0)))
    parts = parts.astype(jnp.bfloat16)
    for j in range(mp_count):
        slot = plan[j]
        for c in range(slots.shape[2] // lanes):
            out[j, c * rows : (c + 1) * rows, :] = slots[slot, :, c * lanes : (c + 1) * lanes]
        out[j, out.shape[1] - 16 :, :] = parts


def pick_kernel(mp_count, per_shard, order, plan, *refs):
    arrived, out = dict(zip(order, refs)), refs[-1]
    shard = lax.axis_index("mp")
    for r in range(per_shard):
        source = plan[mp_count + r] ^ shard
        for d in range(mp_count):

            @pl.when(source == d)
            def _(d=d, r=r):
                out[r] = arrived[d][...]


def precond_kernel(mp_count, per_shard, plan, right_prod, half_sq, arrived, precond, stats, left):
    rows, lanes = left.shape[0], arrived.shape[2]
    stats[...] = jnp.zeros_like(stats)
    stats[per_shard : 2 * per_shard, :] = half_sq[...]
    parts = jnp.sum(arrived[:, arrived.shape[1] - 16 :, :].astype(jnp.float32), axis=0)
    stats[2 * per_shard : 2 * per_shard + 1, :] = jnp.sum(parts, axis=0, keepdims=True)
    for r in range(per_shard):
        source = plan[mp_count + r]
        for c in range(left.shape[1] // lanes):
            left[:, c * lanes : (c + 1) * lanes] = arrived[source, c * rows : (c + 1) * rows, :]
        product = jnp.dot(left[...], right_prod[r], preferred_element_type=jnp.float32)
        precond[r] = product
        total = jnp.sum(jnp.sum(product * product, axis=1, keepdims=True), axis=0, keepdims=True)
        stats[r : r + 1, :] = jnp.broadcast_to(total, (1, lanes))


def finish_kernel(area, cells, precond, *refs):
    parts, update = refs[:-1], refs[-1]
    per_shard = update.shape[0]
    total = parts[0][...]
    for part in parts[1:]:
        total += part[...]
    precond_sq, block_sq = total[:per_shard], total[per_shard : 2 * per_shard]
    square_total = total[2 * per_shard : 2 * per_shard + 1]
    graft = jnp.sqrt(block_sq / area + epsilon) / jnp.sqrt(precond_sq / area + epsilon)
    scale = max_rms / jnp.sqrt(square_total / cells + epsilon) * graft
    for r in range(per_shard):
        update[r] = (scale[r : r + 1, :1] * precond[r]).astype(update.dtype)


def shards(grad_partials, owner_lists, owner_offsets, left_roots, right_roots):
    dp_count = lax.axis_size("dp")
    mp_count = lax.axis_size("mp")
    dp_index = lax.axis_index("dp")
    partial_blocks = grad_partials[0]
    per_shard = partial_blocks.shape[0]
    width = partial_blocks.shape[2]
    rows = width // dp_count
    area = width * width
    cells = owner_lists.shape[0] * area
    piece = jax.ShapeDtypeStruct((rows, width), jnp.bfloat16)
    lanes = 128

    params = pltpu.CompilerParams(vmem_limit_bytes=16 * 2**20)

    def over_dp(factor):
        return lax.all_to_all(
            factor[0, 0].reshape(dp_count, rows, width), "dp", split_axis=0, concat_axis=0, tiled=True
        )

    plan = pl.pallas_call(
        functools.partial(plan_kernel, mp_count, per_shard),
        out_shape=jax.ShapeDtypeStruct((mp_count + per_shard,), jnp.int32),
        in_specs=[SMEM, SMEM],
        out_specs=SMEM,
        compiler_params=params,
    )(owner_lists, owner_offsets)
    right_slots = over_dp(right_roots)
    total = core_sum(partial_blocks, dp_index)
    right_slots, total, plan = lax.optimization_barrier((right_slots, total, plan))
    outgoing = pl.pallas_call(
        functools.partial(right_kernel, mp_count),
        out_shape=[piece] * mp_count,
        in_specs=[SMEM, VMEM],
        out_specs=[VMEM] * mp_count,
        compiler_params=params,
    )(plan, right_slots)
    left_slots = over_dp(left_roots)
    far = mp_count // 2
    order = [1, far, *range(2, far), *range(far + 1, mp_count)]
    right_arrived = [outgoing[0]] + [swap(outgoing[d], "mp", d) for d in order]
    total = chip_sum(total, dp_count, dp_index)
    total_f = total.astype(jnp.float32)
    half_sq = jnp.broadcast_to(
        jnp.sum(total_f * total_f, axis=(1, 2)).reshape(per_shard, 1),
        (per_shard, lanes),
    )
    left_outgoing = pl.pallas_call(
        functools.partial(left_kernel, mp_count),
        out_shape=jax.ShapeDtypeStruct((mp_count, rows * width // lanes + 16, lanes), jnp.bfloat16),
        in_specs=[SMEM, VMEM, VMEM],
        out_specs=VMEM,
        compiler_params=params,
    )(plan, left_slots, half_sq)
    left_arrived = lax.all_to_all(left_outgoing, "mp", split_axis=0, concat_axis=0, tiled=True)
    right_rows = pl.pallas_call(
        functools.partial(pick_kernel, mp_count, per_shard, [0] + order),
        out_shape=jax.ShapeDtypeStruct((per_shard, rows, width), jnp.bfloat16),
        in_specs=[SMEM] + [VMEM] * mp_count + [ANY],
        out_specs=VMEM,
        compiler_params=params,
    )(plan, *right_arrived, left_outgoing)
    right = gather_rows(right_rows, dp_count, dp_index)

    grad = whole_rows(total, dp_count, dp_index)
    right_prod = jnp.einsum(
        "bij,bjk->bik", grad, right, preferred_element_type=jnp.float32
    ).astype(jnp.bfloat16)
    precond, stats = pl.pallas_call(
        functools.partial(precond_kernel, mp_count, per_shard),
        out_shape=[
            jax.ShapeDtypeStruct((per_shard, rows, width), jnp.float32),
            jax.ShapeDtypeStruct((pl.cdiv(2 * per_shard + 1, 8) * 8, lanes), jnp.float32),
        ],
        in_specs=[SMEM, VMEM, VMEM, VMEM],
        out_specs=[VMEM, VMEM],
        scratch_shapes=[pltpu.VMEM((rows, width), jnp.bfloat16)],
        compiler_params=params,
    )(plan, right_prod, half_sq, left_arrived)
    parts = [stats] + [swap(stats, "dp", d) for d in range(1, dp_count)]
    return pl.pallas_call(
        functools.partial(finish_kernel, area, cells),
        out_shape=jax.ShapeDtypeStruct((per_shard, rows, width), jnp.bfloat16),
        in_specs=[VMEM] * (1 + dp_count),
        out_specs=VMEM,
        compiler_params=params,
    )(precond, *parts)


def solution(mesh):
    return jax.shard_map(
        shards,
        mesh=mesh,
        in_specs=(
            P("dp", "mp", None, None),
            P(),
            P(),
            P("mp", "dp", None, None),
            P("mp", "dp", None, None),
        ),
        out_specs=P("mp", "dp", None),
        check_vma=False,
    )
```

```python
import functools

import jax
import jax.numpy as jnp
from jax import lax
from jax.experimental import pallas as pl
from jax.experimental.pallas import tpu as pltpu
from jax.sharding import PartitionSpec as P

epsilon = 1e-06
max_rms = 1.0

SMEM = pl.BlockSpec(memory_space=pltpu.SMEM)
VMEM = pl.BlockSpec(memory_space=pltpu.VMEM)
ANY = pl.BlockSpec(memory_space=pl.ANY)


def swap(value, axis, distance):
    count = lax.axis_size(axis)
    return lax.ppermute(value, axis, [(i, i ^ distance) for i in range(count)])


def add_rounded(a, b):
    return (a.astype(jnp.float32) + b.astype(jnp.float32)).astype(jnp.bfloat16)


def core_sum(partial_blocks, dp_index):
    half = partial_blocks.shape[1] // 2
    core = dp_index % 2
    other = swap(partial_blocks, "dp", 1)
    kept = lax.dynamic_slice_in_dim(partial_blocks, core * half, half, axis=1)
    taken = lax.dynamic_slice_in_dim(other, core * half, half, axis=1)
    return add_rounded(kept, taken)


def chip_sum(total, dp_count, dp_index):
    distance = 2
    while distance < dp_count:
        part = total.shape[1] // 2
        bit = (dp_index // distance) % 2
        kept = lax.dynamic_slice_in_dim(total, bit * part, part, axis=1)
        given = lax.dynamic_slice_in_dim(total, (1 - bit) * part, part, axis=1)
        total = add_rounded(kept, swap(given, "dp", distance))
        distance *= 2
    return total


def whole_rows(total, dp_count, dp_index):
    part = total.shape[1]
    pieces, distance = {0: total}, dp_count // 2
    while distance >= 1:
        pieces |= {d ^ distance: swap(piece, "dp", distance) for d, piece in pieces.items()}
        distance //= 2
    whole = jnp.zeros((total.shape[0], part * dp_count, total.shape[2]), total.dtype)
    for d, piece in pieces.items():
        holder, place, distance = dp_index ^ d, 0, 1
        while distance < dp_count:
            place = 2 * place + (holder // distance) % 2
            distance *= 2
        whole = lax.dynamic_update_slice_in_dim(whole, piece, place * part, axis=1)
    return whole


def gather_rows(rows, dp_count, dp_index):
    per_shard, _, width = rows.shape
    parts = rows[:, None]
    distance = dp_count // 2
    while distance >= 1:
        other = swap(parts, "dp", distance)
        bit = (dp_index // distance) % 2
        low = jnp.where(bit == 0, parts, other)
        high = jnp.where(bit == 0, other, parts)
        parts = jnp.stack([low, high], axis=2)
        parts = parts.reshape(per_shard, -1, *rows.shape[1:])
        distance //= 2
    return parts.reshape(per_shard, -1, width)


def plan_kernel(mp_count, per_shard, lists, offsets, plan):
    column = lax.axis_index("mp")
    start = offsets[column]
    for j in range(mp_count):
        plan[j] = 0

    def note(p, carry):
        plan[lists[p] // per_shard] = p - start
        return carry

    lax.fori_loop(start, offsets[column + 1], note, 0)

    def owner(p, carry):
        block = lists[p]

        @pl.when(block // per_shard == column)
        def _():
            plan[mp_count + block % per_shard] = lax.fori_loop(
                0, mp_count, lambda c, total: total + (offsets[c + 1] <= p).astype(jnp.int32), 0
            )

        return carry

    lax.fori_loop(0, lists.shape[0], owner, 0)


def right_kernel(mp_count, plan, slots, *outs):
    column = lax.axis_index("mp")
    for d in range(mp_count):
        outs[d][...] = slots[plan[column ^ d]]


def left_kernel(mp_count, plan, slots, half_sq, out):
    rows = slots.shape[1]
    lanes = out.shape[2]
    total = jnp.sum(half_sq[...], axis=0, keepdims=True)
    first = total.astype(jnp.bfloat16).astype(jnp.float32)
    second = (total - first).astype(jnp.bfloat16).astype(jnp.float32)
    third = total - first - second
    row = lax.broadcasted_iota(jnp.int32, (16, lanes), 0)
    parts = jnp.where(row == 0, first, jnp.where(row == 1, second, jnp.where(row == 2, third, 0.0)))
    parts = parts.astype(jnp.bfloat16)
    for j in range(mp_count):
        slot = plan[j]
        for c in range(slots.shape[2] // lanes):
            out[j, c * rows : (c + 1) * rows, :] = slots[slot, :, c * lanes : (c + 1) * lanes]
        out[j, out.shape[1] - 16 :, :] = parts


def pick_kernel(mp_count, per_shard, order, plan, *refs):
    arrived, out = dict(zip(order, refs)), refs[-1]
    shard = lax.axis_index("mp")
    for r in range(per_shard):
        source = plan[mp_count + r] ^ shard
        for d in range(mp_count):

            @pl.when(source == d)
            def _(d=d, r=r):
                out[r] = arrived[d][...]


def precond_kernel(mp_count, per_shard, plan, right_prod, half_sq, arrived, precond, stats, left):
    rows, lanes = left.shape[0], arrived.shape[2]
    stats[...] = jnp.zeros_like(stats)
    stats[per_shard : 2 * per_shard, :] = half_sq[...]
    parts = jnp.sum(arrived[:, arrived.shape[1] - 16 :, :].astype(jnp.float32), axis=0)
    stats[2 * per_shard : 2 * per_shard + 1, :] = jnp.sum(parts, axis=0, keepdims=True)
    for r in range(per_shard):
        source = plan[mp_count + r]
        for c in range(left.shape[1] // lanes):
            left[:, c * lanes : (c + 1) * lanes] = arrived[source, c * rows : (c + 1) * rows, :]
        product = jnp.dot(left[...], right_prod[r], preferred_element_type=jnp.float32)
        precond[r] = product
        total = jnp.sum(jnp.sum(product * product, axis=1, keepdims=True), axis=0, keepdims=True)
        stats[r : r + 1, :] = jnp.broadcast_to(total, (1, lanes))


def finish_kernel(area, cells, precond, *refs):
    parts, update = refs[:-1], refs[-1]
    per_shard = update.shape[0]
    total = parts[0][...]
    for part in parts[1:]:
        total += part[...]
    precond_sq, block_sq = total[:per_shard], total[per_shard : 2 * per_shard]
    square_total = total[2 * per_shard : 2 * per_shard + 1]
    graft = jnp.sqrt(block_sq / area + epsilon) / jnp.sqrt(precond_sq / area + epsilon)
    scale = max_rms / jnp.sqrt(square_total / cells + epsilon) * graft
    for r in range(per_shard):
        update[r] = (scale[r : r + 1, :1] * precond[r]).astype(update.dtype)


def shards(grad_partials, owner_lists, owner_offsets, left_roots, right_roots):
    dp_count = lax.axis_size("dp")
    mp_count = lax.axis_size("mp")
    dp_index = lax.axis_index("dp")
    partial_blocks = grad_partials[0]
    per_shard = partial_blocks.shape[0]
    width = partial_blocks.shape[2]
    rows = width // dp_count
    area = width * width
    cells = owner_lists.shape[0] * area
    piece = jax.ShapeDtypeStruct((rows, width), jnp.bfloat16)
    lanes = 128

    params = pltpu.CompilerParams(vmem_limit_bytes=16 * 2**20)

    def over_dp(factor):
        return lax.all_to_all(
            factor[0, 0].reshape(dp_count, rows, width), "dp", split_axis=0, concat_axis=0, tiled=True
        )

    plan = pl.pallas_call(
        functools.partial(plan_kernel, mp_count, per_shard),
        out_shape=jax.ShapeDtypeStruct((mp_count + per_shard,), jnp.int32),
        in_specs=[SMEM, SMEM],
        out_specs=SMEM,
        compiler_params=params,
    )(owner_lists, owner_offsets)
    right_slots = over_dp(right_roots)
    total = core_sum(partial_blocks, dp_index)
    right_slots, total, plan = lax.optimization_barrier((right_slots, total, plan))
    outgoing = pl.pallas_call(
        functools.partial(right_kernel, mp_count),
        out_shape=[piece] * mp_count,
        in_specs=[SMEM, VMEM],
        out_specs=[VMEM] * mp_count,
        compiler_params=params,
    )(plan, right_slots)
    left_slots = over_dp(left_roots)
    far = mp_count // 2
    middle = far + far // 2
    distant = [*range(middle, mp_count), *range(far, middle)]
    order = [1, distant[0], *range(2, far), *distant[1:]]
    right_arrived = [outgoing[0]] + [swap(outgoing[d], "mp", d) for d in order]
    total = chip_sum(total, dp_count, dp_index)
    total_f = total.astype(jnp.float32)
    half_sq = jnp.broadcast_to(
        jnp.sum(total_f * total_f, axis=(1, 2)).reshape(per_shard, 1),
        (per_shard, lanes),
    )
    left_outgoing = pl.pallas_call(
        functools.partial(left_kernel, mp_count),
        out_shape=jax.ShapeDtypeStruct((mp_count, rows * width // lanes + 16, lanes), jnp.bfloat16),
        in_specs=[SMEM, VMEM, VMEM],
        out_specs=VMEM,
        compiler_params=params,
    )(plan, left_slots, half_sq)
    left_arrived = lax.all_to_all(left_outgoing, "mp", split_axis=0, concat_axis=0, tiled=True)
    right_rows = pl.pallas_call(
        functools.partial(pick_kernel, mp_count, per_shard, [0] + order),
        out_shape=jax.ShapeDtypeStruct((per_shard, rows, width), jnp.bfloat16),
        in_specs=[SMEM] + [VMEM] * mp_count + [ANY],
        out_specs=VMEM,
        compiler_params=params,
    )(plan, *right_arrived, left_outgoing)
    right = gather_rows(right_rows, dp_count, dp_index)

    grad = whole_rows(total, dp_count, dp_index)
    right_prod = jnp.einsum(
        "bij,bjk->bik", grad, right, preferred_element_type=jnp.float32
    ).astype(jnp.bfloat16)
    precond, stats = pl.pallas_call(
        functools.partial(precond_kernel, mp_count, per_shard),
        out_shape=[
            jax.ShapeDtypeStruct((per_shard, rows, width), jnp.float32),
            jax.ShapeDtypeStruct((pl.cdiv(2 * per_shard + 1, 8) * 8, lanes), jnp.float32),
        ],
        in_specs=[SMEM, VMEM, VMEM, VMEM],
        out_specs=[VMEM, VMEM],
        scratch_shapes=[pltpu.VMEM((rows, width), jnp.bfloat16)],
        compiler_params=params,
    )(plan, right_prod, half_sq, left_arrived)
    parts = [stats] + [swap(stats, "dp", d) for d in range(1, dp_count)]
    return pl.pallas_call(
        functools.partial(finish_kernel, area, cells),
        out_shape=jax.ShapeDtypeStruct((per_shard, rows, width), jnp.bfloat16),
        in_specs=[VMEM] * (1 + dp_count),
        out_specs=VMEM,
        compiler_params=params,
    )(precond, *parts)


def solution(mesh):
    return jax.shard_map(
        shards,
        mesh=mesh,
        in_specs=(
            P("dp", "mp", None, None),
            P(),
            P(),
            P("mp", "dp", None, None),
            P("mp", "dp", None, None),
        ),
        out_specs=P("mp", "dp", None),
        check_vma=False,
    )
```

```python
import functools

import jax
import jax.numpy as jnp
from jax import lax
from jax.experimental import pallas as pl
from jax.experimental.pallas import tpu as pltpu
from jax.sharding import PartitionSpec as P

epsilon = 1e-06
max_rms = 1.0

SMEM = pl.BlockSpec(memory_space=pltpu.SMEM)
VMEM = pl.BlockSpec(memory_space=pltpu.VMEM)
ANY = pl.BlockSpec(memory_space=pl.ANY)


def swap(value, axis, distance):
    count = lax.axis_size(axis)
    return lax.ppermute(value, axis, [(i, i ^ distance) for i in range(count)])


def add_rounded(a, b):
    return (a.astype(jnp.float32) + b.astype(jnp.float32)).astype(jnp.bfloat16)


def core_sum(partial_blocks, dp_index):
    half = partial_blocks.shape[1] // 2
    core = dp_index % 2
    other = swap(partial_blocks, "dp", 1)
    kept = lax.dynamic_slice_in_dim(partial_blocks, core * half, half, axis=1)
    taken = lax.dynamic_slice_in_dim(other, core * half, half, axis=1)
    return add_rounded(kept, taken)


def chip_sum(total, dp_count, dp_index):
    distance = 2
    while distance < dp_count:
        part = total.shape[1] // 2
        bit = (dp_index // distance) % 2
        kept = lax.dynamic_slice_in_dim(total, bit * part, part, axis=1)
        given = lax.dynamic_slice_in_dim(total, (1 - bit) * part, part, axis=1)
        total = add_rounded(kept, swap(given, "dp", distance))
        distance *= 2
    return total


def whole_rows(total, dp_count, dp_index):
    part = total.shape[1]
    pieces, distance = {0: total}, dp_count // 2
    while distance >= 1:
        pieces |= {d ^ distance: swap(piece, "dp", distance) for d, piece in pieces.items()}
        distance //= 2
    whole = jnp.zeros((total.shape[0], part * dp_count, total.shape[2]), total.dtype)
    for d, piece in pieces.items():
        holder, place, distance = dp_index ^ d, 0, 1
        while distance < dp_count:
            place = 2 * place + (holder // distance) % 2
            distance *= 2
        whole = lax.dynamic_update_slice_in_dim(whole, piece, place * part, axis=1)
    return whole


def gather_rows(rows, dp_count, dp_index):
    per_shard, _, width = rows.shape
    parts = rows[:, None]
    distance = dp_count // 2
    while distance >= 1:
        other = swap(parts, "dp", distance)
        bit = (dp_index // distance) % 2
        low = jnp.where(bit == 0, parts, other)
        high = jnp.where(bit == 0, other, parts)
        parts = jnp.stack([low, high], axis=2)
        parts = parts.reshape(per_shard, -1, *rows.shape[1:])
        distance //= 2
    return parts.reshape(per_shard, -1, width)


def plan_kernel(mp_count, per_shard, lists, offsets, plan):
    column = lax.axis_index("mp")
    start = offsets[column]
    for j in range(mp_count):
        plan[j] = 0

    def note(p, carry):
        plan[lists[p] // per_shard] = p - start
        return carry

    lax.fori_loop(start, offsets[column + 1], note, 0)

    def owner(p, carry):
        block = lists[p]

        @pl.when(block // per_shard == column)
        def _():
            plan[mp_count + block % per_shard] = lax.fori_loop(
                0, mp_count, lambda c, total: total + (offsets[c + 1] <= p).astype(jnp.int32), 0
            )

        return carry

    lax.fori_loop(0, lists.shape[0], owner, 0)


def right_kernel(mp_count, plan, slots, *outs):
    column = lax.axis_index("mp")
    for d in range(mp_count):
        outs[d][...] = slots[plan[column ^ d]]


def left_kernel(mp_count, plan, slots, half_sq, out):
    rows = slots.shape[1]
    lanes = out.shape[2]
    total = jnp.sum(half_sq[...], axis=0, keepdims=True)
    first = total.astype(jnp.bfloat16).astype(jnp.float32)
    second = (total - first).astype(jnp.bfloat16).astype(jnp.float32)
    third = total - first - second
    row = lax.broadcasted_iota(jnp.int32, (16, lanes), 0)
    parts = jnp.where(row == 0, first, jnp.where(row == 1, second, jnp.where(row == 2, third, 0.0)))
    parts = parts.astype(jnp.bfloat16)
    for j in range(mp_count):
        slot = plan[j]
        for c in range(slots.shape[2] // lanes):
            out[j, c * rows : (c + 1) * rows, :] = slots[slot, :, c * lanes : (c + 1) * lanes]
        out[j, out.shape[1] - 16 :, :] = parts


def pick_kernel(mp_count, per_shard, order, plan, *refs):
    arrived, out = dict(zip(order, refs)), refs[-1]
    shard = lax.axis_index("mp")
    for r in range(per_shard):
        source = plan[mp_count + r] ^ shard
        for d in range(mp_count):

            @pl.when(source == d)
            def _(d=d, r=r):
                out[r] = arrived[d][...]


def precond_kernel(mp_count, per_shard, plan, right_prod, half_sq, arrived, precond, stats, left):
    rows, lanes = left.shape[0], arrived.shape[2]
    stats[...] = jnp.zeros_like(stats)
    stats[per_shard : 2 * per_shard, :] = half_sq[...]
    parts = jnp.sum(arrived[:, arrived.shape[1] - 16 :, :].astype(jnp.float32), axis=0)
    stats[2 * per_shard : 2 * per_shard + 1, :] = jnp.sum(parts, axis=0, keepdims=True)
    for r in range(per_shard):
        source = plan[mp_count + r]
        for c in range(left.shape[1] // lanes):
            left[:, c * lanes : (c + 1) * lanes] = arrived[source, c * rows : (c + 1) * rows, :]
        product = jnp.dot(left[...], right_prod[r], preferred_element_type=jnp.float32)
        precond[r] = product
        total = jnp.sum(jnp.sum(product * product, axis=1, keepdims=True), axis=0, keepdims=True)
        stats[r : r + 1, :] = jnp.broadcast_to(total, (1, lanes))


def finish_kernel(area, cells, precond, *refs):
    parts, update = refs[:-1], refs[-1]
    per_shard = update.shape[0]
    total = parts[0][...]
    for part in parts[1:]:
        total += part[...]
    precond_sq, block_sq = total[:per_shard], total[per_shard : 2 * per_shard]
    square_total = total[2 * per_shard : 2 * per_shard + 1]
    graft = jnp.sqrt(block_sq / area + epsilon) / jnp.sqrt(precond_sq / area + epsilon)
    scale = max_rms / jnp.sqrt(square_total / cells + epsilon) * graft
    for r in range(per_shard):
        update[r] = (scale[r : r + 1, :1] * precond[r]).astype(update.dtype)


def shards(grad_partials, owner_lists, owner_offsets, left_roots, right_roots):
    dp_count = lax.axis_size("dp")
    mp_count = lax.axis_size("mp")
    dp_index = lax.axis_index("dp")
    partial_blocks = grad_partials[0]
    per_shard = partial_blocks.shape[0]
    width = partial_blocks.shape[2]
    rows = width // dp_count
    area = width * width
    cells = owner_lists.shape[0] * area
    piece = jax.ShapeDtypeStruct((rows, width), jnp.bfloat16)
    lanes = 128

    params = pltpu.CompilerParams(vmem_limit_bytes=16 * 2**20)

    def over_dp(factor):
        return lax.all_to_all(
            factor[0, 0].reshape(dp_count, rows, width), "dp", split_axis=0, concat_axis=0, tiled=True
        )

    plan = pl.pallas_call(
        functools.partial(plan_kernel, mp_count, per_shard),
        out_shape=jax.ShapeDtypeStruct((mp_count + per_shard,), jnp.int32),
        in_specs=[SMEM, SMEM],
        out_specs=SMEM,
        compiler_params=params,
    )(owner_lists, owner_offsets)
    right_slots = over_dp(right_roots)
    total = core_sum(partial_blocks, dp_index)
    right_slots, total, plan = lax.optimization_barrier((right_slots, total, plan))
    outgoing = pl.pallas_call(
        functools.partial(right_kernel, mp_count),
        out_shape=[piece] * mp_count,
        in_specs=[SMEM, VMEM],
        out_specs=[VMEM] * mp_count,
        compiler_params=params,
    )(plan, right_slots)
    left_slots = over_dp(left_roots)
    far = mp_count // 2
    middle = far + far // 2
    distant = [d for pair in zip(range(middle, mp_count), range(far, middle)) for d in pair]
    order = [1, distant[0], *range(2, far), *distant[1:]]
    right_arrived = [outgoing[0]] + [swap(outgoing[d], "mp", d) for d in order]
    total = chip_sum(total, dp_count, dp_index)
    total_f = total.astype(jnp.float32)
    half_sq = jnp.broadcast_to(
        jnp.sum(total_f * total_f, axis=(1, 2)).reshape(per_shard, 1),
        (per_shard, lanes),
    )
    left_outgoing = pl.pallas_call(
        functools.partial(left_kernel, mp_count),
        out_shape=jax.ShapeDtypeStruct((mp_count, rows * width // lanes + 16, lanes), jnp.bfloat16),
        in_specs=[SMEM, VMEM, VMEM],
        out_specs=VMEM,
        compiler_params=params,
    )(plan, left_slots, half_sq)
    left_arrived = lax.all_to_all(left_outgoing, "mp", split_axis=0, concat_axis=0, tiled=True)
    right_rows = pl.pallas_call(
        functools.partial(pick_kernel, mp_count, per_shard, [0] + order),
        out_shape=jax.ShapeDtypeStruct((per_shard, rows, width), jnp.bfloat16),
        in_specs=[SMEM] + [VMEM] * mp_count + [ANY],
        out_specs=VMEM,
        compiler_params=params,
    )(plan, *right_arrived, left_outgoing)
    right = gather_rows(right_rows, dp_count, dp_index)

    grad = whole_rows(total, dp_count, dp_index)
    right_prod = jnp.einsum(
        "bij,bjk->bik", grad, right, preferred_element_type=jnp.float32
    ).astype(jnp.bfloat16)
    precond, stats = pl.pallas_call(
        functools.partial(precond_kernel, mp_count, per_shard),
        out_shape=[
            jax.ShapeDtypeStruct((per_shard, rows, width), jnp.float32),
            jax.ShapeDtypeStruct((pl.cdiv(2 * per_shard + 1, 8) * 8, lanes), jnp.float32),
        ],
        in_specs=[SMEM, VMEM, VMEM, VMEM],
        out_specs=[VMEM, VMEM],
        scratch_shapes=[pltpu.VMEM((rows, width), jnp.bfloat16)],
        compiler_params=params,
    )(plan, right_prod, half_sq, left_arrived)
    parts = [stats] + [swap(stats, "dp", d) for d in range(1, dp_count)]
    return pl.pallas_call(
        functools.partial(finish_kernel, area, cells),
        out_shape=jax.ShapeDtypeStruct((per_shard, rows, width), jnp.bfloat16),
        in_specs=[VMEM] * (1 + dp_count),
        out_specs=VMEM,
        compiler_params=params,
    )(precond, *parts)


def solution(mesh):
    return jax.shard_map(
        shards,
        mesh=mesh,
        in_specs=(
            P("dp", "mp", None, None),
            P(),
            P(),
            P("mp", "dp", None, None),
            P("mp", "dp", None, None),
        ),
        out_specs=P("mp", "dp", None),
        check_vma=False,
    )
```

```python
import functools

import jax
import jax.numpy as jnp
from jax import lax
from jax.experimental import pallas as pl
from jax.experimental.pallas import tpu as pltpu
from jax.sharding import PartitionSpec as P

epsilon = 1e-06
max_rms = 1.0

SMEM = pl.BlockSpec(memory_space=pltpu.SMEM)
VMEM = pl.BlockSpec(memory_space=pltpu.VMEM)
ANY = pl.BlockSpec(memory_space=pl.ANY)


def swap(value, axis, distance):
    count = lax.axis_size(axis)
    return lax.ppermute(value, axis, [(i, i ^ distance) for i in range(count)])


def add_rounded(a, b):
    return (a.astype(jnp.float32) + b.astype(jnp.float32)).astype(jnp.bfloat16)


def core_sum(partial_blocks, dp_index):
    half = partial_blocks.shape[1] // 2
    core = dp_index % 2
    other = swap(partial_blocks, "dp", 1)
    kept = lax.dynamic_slice_in_dim(partial_blocks, core * half, half, axis=1)
    taken = lax.dynamic_slice_in_dim(other, core * half, half, axis=1)
    return add_rounded(kept, taken)


def chip_sum(total, dp_count, dp_index):
    distance = 2
    while distance < dp_count:
        part = total.shape[1] // 2
        bit = (dp_index // distance) % 2
        kept = lax.dynamic_slice_in_dim(total, bit * part, part, axis=1)
        given = lax.dynamic_slice_in_dim(total, (1 - bit) * part, part, axis=1)
        total = add_rounded(kept, swap(given, "dp", distance))
        distance *= 2
    return total


def whole_rows(total, dp_count, dp_index):
    part = total.shape[1]
    pieces, distance = {0: total}, dp_count // 2
    while distance >= 1:
        pieces |= {d ^ distance: swap(piece, "dp", distance) for d, piece in pieces.items()}
        distance //= 2
    whole = jnp.zeros((total.shape[0], part * dp_count, total.shape[2]), total.dtype)
    for d, piece in pieces.items():
        holder, place, distance = dp_index ^ d, 0, 1
        while distance < dp_count:
            place = 2 * place + (holder // distance) % 2
            distance *= 2
        whole = lax.dynamic_update_slice_in_dim(whole, piece, place * part, axis=1)
    return whole


def gather_rows(rows, dp_count, dp_index):
    per_shard, _, width = rows.shape
    parts = rows[:, None]
    distance = dp_count // 2
    while distance >= 1:
        other = swap(parts, "dp", distance)
        bit = (dp_index // distance) % 2
        low = jnp.where(bit == 0, parts, other)
        high = jnp.where(bit == 0, other, parts)
        parts = jnp.stack([low, high], axis=2)
        parts = parts.reshape(per_shard, -1, *rows.shape[1:])
        distance //= 2
    return parts.reshape(per_shard, -1, width)


def plan_kernel(mp_count, per_shard, lists, offsets, plan):
    column = lax.axis_index("mp")
    start = offsets[column]
    for j in range(mp_count):
        plan[j] = 0

    def note(p, carry):
        plan[lists[p] // per_shard] = p - start
        return carry

    lax.fori_loop(start, offsets[column + 1], note, 0)

    def owner(p, carry):
        block = lists[p]

        @pl.when(block // per_shard == column)
        def _():
            plan[mp_count + block % per_shard] = lax.fori_loop(
                0, mp_count, lambda c, total: total + (offsets[c + 1] <= p).astype(jnp.int32), 0
            )

        return carry

    lax.fori_loop(0, lists.shape[0], owner, 0)


def right_kernel(mp_count, plan, slots, *outs):
    column = lax.axis_index("mp")
    for d in range(mp_count):
        outs[d][...] = slots[plan[column ^ d]]


def left_kernel(mp_count, plan, slots, own_rows, out, half_sq):
    rows = slots.shape[1]
    lanes = out.shape[2]
    total = jnp.zeros((1, lanes), jnp.float32)
    for r in range(own_rows.shape[0]):
        block = own_rows[r].astype(jnp.float32)
        square = jnp.sum(jnp.sum(block * block, axis=1, keepdims=True), axis=0, keepdims=True)
        half_sq[r : r + 1, :] = jnp.broadcast_to(square, (1, lanes))
        total += square
    first = total.astype(jnp.bfloat16).astype(jnp.float32)
    second = (total - first).astype(jnp.bfloat16).astype(jnp.float32)
    third = total - first - second
    row = lax.broadcasted_iota(jnp.int32, (16, lanes), 0)
    parts = jnp.where(row == 0, first, jnp.where(row == 1, second, jnp.where(row == 2, third, 0.0)))
    parts = parts.astype(jnp.bfloat16)
    for j in range(mp_count):
        slot = plan[j]
        for c in range(slots.shape[2] // lanes):
            out[j, c * rows : (c + 1) * rows, :] = slots[slot, :, c * lanes : (c + 1) * lanes]
        out[j, out.shape[1] - 16 :, :] = parts


def pick_kernel(mp_count, per_shard, order, plan, *refs):
    arrived, out = dict(zip(order, refs)), refs[-1]
    shard = lax.axis_index("mp")
    for r in range(per_shard):
        source = plan[mp_count + r] ^ shard
        for d in range(mp_count):

            @pl.when(source == d)
            def _(d=d, r=r):
                out[r] = arrived[d][...]


def precond_kernel(mp_count, per_shard, plan, right_prod, half_sq, arrived, precond, stats, left):
    rows, lanes = left.shape[0], arrived.shape[2]
    stats[...] = jnp.zeros_like(stats)
    stats[per_shard : 2 * per_shard, :] = half_sq[...]
    parts = jnp.sum(arrived[:, arrived.shape[1] - 16 :, :].astype(jnp.float32), axis=0)
    stats[2 * per_shard : 2 * per_shard + 1, :] = jnp.sum(parts, axis=0, keepdims=True)
    for r in range(per_shard):
        source = plan[mp_count + r]
        for c in range(left.shape[1] // lanes):
            left[:, c * lanes : (c + 1) * lanes] = arrived[source, c * rows : (c + 1) * rows, :]
        product = jnp.dot(left[...], right_prod[r], preferred_element_type=jnp.float32)
        precond[r] = product
        total = jnp.sum(jnp.sum(product * product, axis=1, keepdims=True), axis=0, keepdims=True)
        stats[r : r + 1, :] = jnp.broadcast_to(total, (1, lanes))


def finish_kernel(area, cells, precond, *refs):
    parts, update = refs[:-1], refs[-1]
    per_shard = update.shape[0]
    total = parts[0][...]
    for part in parts[1:]:
        total += part[...]
    precond_sq, block_sq = total[:per_shard], total[per_shard : 2 * per_shard]
    square_total = total[2 * per_shard : 2 * per_shard + 1]
    graft = jnp.sqrt(block_sq / area + epsilon) / jnp.sqrt(precond_sq / area + epsilon)
    scale = max_rms / jnp.sqrt(square_total / cells + epsilon) * graft
    for r in range(per_shard):
        update[r] = (scale[r : r + 1, :1] * precond[r]).astype(update.dtype)


def shards(grad_partials, owner_lists, owner_offsets, left_roots, right_roots):
    dp_count = lax.axis_size("dp")
    mp_count = lax.axis_size("mp")
    dp_index = lax.axis_index("dp")
    partial_blocks = grad_partials[0]
    per_shard = partial_blocks.shape[0]
    width = partial_blocks.shape[2]
    rows = width // dp_count
    area = width * width
    cells = owner_lists.shape[0] * area
    piece = jax.ShapeDtypeStruct((rows, width), jnp.bfloat16)
    lanes = 128

    params = pltpu.CompilerParams(vmem_limit_bytes=16 * 2**20)

    def over_dp(factor):
        return lax.all_to_all(
            factor[0, 0].reshape(dp_count, rows, width), "dp", split_axis=0, concat_axis=0, tiled=True
        )

    plan = pl.pallas_call(
        functools.partial(plan_kernel, mp_count, per_shard),
        out_shape=jax.ShapeDtypeStruct((mp_count + per_shard,), jnp.int32),
        in_specs=[SMEM, SMEM],
        out_specs=SMEM,
        compiler_params=params,
    )(owner_lists, owner_offsets)
    right_slots = over_dp(right_roots)
    total = core_sum(partial_blocks, dp_index)
    right_slots, total, plan = lax.optimization_barrier((right_slots, total, plan))
    outgoing = pl.pallas_call(
        functools.partial(right_kernel, mp_count),
        out_shape=[piece] * mp_count,
        in_specs=[SMEM, VMEM],
        out_specs=[VMEM] * mp_count,
        compiler_params=params,
    )(plan, right_slots)
    left_slots = over_dp(left_roots)
    far = mp_count // 2
    middle = far + far // 2
    distant = [d for pair in zip(range(middle, mp_count), range(far, middle)) for d in pair]
    order = [1, distant[0], *range(2, far), *distant[1:]]
    right_arrived = [outgoing[0]] + [swap(outgoing[d], "mp", d) for d in order]
    total = chip_sum(total, dp_count, dp_index)
    left_outgoing, half_sq = pl.pallas_call(
        functools.partial(left_kernel, mp_count),
        out_shape=[
            jax.ShapeDtypeStruct((mp_count, rows * width // lanes + 16, lanes), jnp.bfloat16),
            jax.ShapeDtypeStruct((per_shard, lanes), jnp.float32),
        ],
        in_specs=[SMEM, VMEM, VMEM],
        out_specs=[VMEM, VMEM],
        compiler_params=params,
    )(plan, left_slots, total)
    left_arrived = lax.all_to_all(left_outgoing, "mp", split_axis=0, concat_axis=0, tiled=True)
    right_rows = pl.pallas_call(
        functools.partial(pick_kernel, mp_count, per_shard, [0] + order),
        out_shape=jax.ShapeDtypeStruct((per_shard, rows, width), jnp.bfloat16),
        in_specs=[SMEM] + [VMEM] * mp_count + [ANY],
        out_specs=VMEM,
        compiler_params=params,
    )(plan, *right_arrived, left_outgoing)
    right = gather_rows(right_rows, dp_count, dp_index)

    grad = whole_rows(total, dp_count, dp_index)
    right_prod = jnp.einsum(
        "bij,bjk->bik", grad, right, preferred_element_type=jnp.float32
    ).astype(jnp.bfloat16)
    precond, stats = pl.pallas_call(
        functools.partial(precond_kernel, mp_count, per_shard),
        out_shape=[
            jax.ShapeDtypeStruct((per_shard, rows, width), jnp.float32),
            jax.ShapeDtypeStruct((pl.cdiv(2 * per_shard + 1, 8) * 8, lanes), jnp.float32),
        ],
        in_specs=[SMEM, VMEM, VMEM, VMEM],
        out_specs=[VMEM, VMEM],
        scratch_shapes=[pltpu.VMEM((rows, width), jnp.bfloat16)],
        compiler_params=params,
    )(plan, right_prod, half_sq, left_arrived)
    parts = [stats] + [swap(stats, "dp", d) for d in range(1, dp_count)]
    return pl.pallas_call(
        functools.partial(finish_kernel, area, cells),
        out_shape=jax.ShapeDtypeStruct((per_shard, rows, width), jnp.bfloat16),
        in_specs=[VMEM] * (1 + dp_count),
        out_specs=VMEM,
        compiler_params=params,
    )(precond, *parts)


def solution(mesh):
    return jax.shard_map(
        shards,
        mesh=mesh,
        in_specs=(
            P("dp", "mp", None, None),
            P(),
            P(),
            P("mp", "dp", None, None),
            P("mp", "dp", None, None),
        ),
        out_specs=P("mp", "dp", None),
        check_vma=False,
    )
```

```python
import functools

import jax
import jax.numpy as jnp
from jax import lax
from jax.experimental import pallas as pl
from jax.experimental.pallas import tpu as pltpu
from jax.sharding import PartitionSpec as P

epsilon = 1e-06
max_rms = 1.0

SMEM = pl.BlockSpec(memory_space=pltpu.SMEM)
VMEM = pl.BlockSpec(memory_space=pltpu.VMEM)
ANY = pl.BlockSpec(memory_space=pl.ANY)


def swap(value, axis, distance):
    count = lax.axis_size(axis)
    return lax.ppermute(value, axis, [(i, i ^ distance) for i in range(count)])


def add_rounded(a, b):
    return (a.astype(jnp.float32) + b.astype(jnp.float32)).astype(jnp.bfloat16)


def core_sum(partial_blocks, dp_index):
    half = partial_blocks.shape[1] // 2
    core = dp_index % 2
    other = swap(partial_blocks, "dp", 1)
    kept = lax.dynamic_slice_in_dim(partial_blocks, core * half, half, axis=1)
    taken = lax.dynamic_slice_in_dim(other, core * half, half, axis=1)
    return add_rounded(kept, taken)


def chip_sum(total, dp_count, dp_index):
    distance = 2
    while distance < dp_count:
        part = total.shape[1] // 2
        bit = (dp_index // distance) % 2
        kept = lax.dynamic_slice_in_dim(total, bit * part, part, axis=1)
        given = lax.dynamic_slice_in_dim(total, (1 - bit) * part, part, axis=1)
        total = add_rounded(kept, swap(given, "dp", distance))
        distance *= 2
    return total


def whole_rows(total, dp_count, dp_index):
    part = total.shape[1]
    pieces, distance = {0: total}, dp_count // 2
    while distance >= 1:
        pieces |= {d ^ distance: swap(piece, "dp", distance) for d, piece in pieces.items()}
        distance //= 2
    whole = jnp.zeros((total.shape[0], part * dp_count, total.shape[2]), total.dtype)
    for d, piece in pieces.items():
        holder, place, distance = dp_index ^ d, 0, 1
        while distance < dp_count:
            place = 2 * place + (holder // distance) % 2
            distance *= 2
        whole = lax.dynamic_update_slice_in_dim(whole, piece, place * part, axis=1)
    return whole


def gather_rows(rows, dp_count, dp_index):
    per_shard, _, width = rows.shape
    parts = rows[:, None]
    distance = dp_count // 2
    while distance >= 1:
        other = swap(parts, "dp", distance)
        bit = (dp_index // distance) % 2
        low = jnp.where(bit == 0, parts, other)
        high = jnp.where(bit == 0, other, parts)
        parts = jnp.stack([low, high], axis=2)
        parts = parts.reshape(per_shard, -1, *rows.shape[1:])
        distance //= 2
    return parts.reshape(per_shard, -1, width)


def plan_kernel(mp_count, per_shard, lists, offsets, plan):
    column = lax.axis_index("mp")
    start = offsets[column]
    for j in range(mp_count):
        plan[j] = 0

    def note(p, carry):
        plan[lists[p] // per_shard] = p - start
        return carry

    lax.fori_loop(start, offsets[column + 1], note, 0)

    def owner(p, carry):
        block = lists[p]

        @pl.when(block // per_shard == column)
        def _():
            plan[mp_count + block % per_shard] = lax.fori_loop(
                0, mp_count, lambda c, total: total + (offsets[c + 1] <= p).astype(jnp.int32), 0
            )

        return carry

    lax.fori_loop(0, lists.shape[0], owner, 0)


def right_kernel(mp_count, plan, slots, *outs):
    column = lax.axis_index("mp")
    for d in range(mp_count):
        outs[d][...] = slots[plan[column ^ d]]


def left_kernel(mp_count, plan, slots, half_sq, out):
    rows = slots.shape[1]
    lanes = out.shape[2]
    total = jnp.sum(half_sq[...], axis=0, keepdims=True)
    first = total.astype(jnp.bfloat16).astype(jnp.float32)
    second = (total - first).astype(jnp.bfloat16).astype(jnp.float32)
    third = total - first - second
    row = lax.broadcasted_iota(jnp.int32, (16, lanes), 0)
    parts = jnp.where(row == 0, first, jnp.where(row == 1, second, jnp.where(row == 2, third, 0.0)))
    parts = parts.astype(jnp.bfloat16)
    for j in range(mp_count):
        slot = plan[j]
        for c in range(slots.shape[2] // lanes):
            out[j, c * rows : (c + 1) * rows, :] = slots[slot, :, c * lanes : (c + 1) * lanes]
        out[j, out.shape[1] - 16 :, :] = parts


def pick_kernel(mp_count, per_shard, order, plan, *refs):
    arrived, out = dict(zip(order, refs)), refs[-1]
    shard = lax.axis_index("mp")
    for r in range(per_shard):
        source = plan[mp_count + r] ^ shard
        for d in range(mp_count):

            @pl.when(source == d)
            def _(d=d, r=r):
                out[r] = arrived[d][...]


def precond_kernel(mp_count, per_shard, plan, right_prod, half_sq, arrived, precond, stats, left):
    rows, lanes = left.shape[0], arrived.shape[2]
    stats[...] = jnp.zeros_like(stats)
    stats[per_shard : 2 * per_shard, :] = half_sq[...]
    parts = jnp.sum(arrived[:, arrived.shape[1] - 16 :, :].astype(jnp.float32), axis=0)
    stats[2 * per_shard : 2 * per_shard + 1, :] = jnp.sum(parts, axis=0, keepdims=True)
    for r in range(per_shard):
        source = plan[mp_count + r]
        for c in range(left.shape[1] // lanes):
            left[:, c * lanes : (c + 1) * lanes] = arrived[source, c * rows : (c + 1) * rows, :]
        product = jnp.dot(left[...], right_prod[r], preferred_element_type=jnp.float32)
        precond[r] = product
        total = jnp.sum(jnp.sum(product * product, axis=1, keepdims=True), axis=0, keepdims=True)
        stats[r : r + 1, :] = jnp.broadcast_to(total, (1, lanes))


def finish_kernel(area, cells, precond, *refs):
    parts, update = refs[:-1], refs[-1]
    per_shard = update.shape[0]
    total = parts[0][...]
    for part in parts[1:]:
        total += part[...]
    precond_sq, block_sq = total[:per_shard], total[per_shard : 2 * per_shard]
    square_total = total[2 * per_shard : 2 * per_shard + 1]
    graft = jnp.sqrt(block_sq / area + epsilon) / jnp.sqrt(precond_sq / area + epsilon)
    scale = max_rms / jnp.sqrt(square_total / cells + epsilon) * graft
    for r in range(per_shard):
        update[r] = (scale[r : r + 1, :1] * precond[r]).astype(update.dtype)


def shards(grad_partials, owner_lists, owner_offsets, left_roots, right_roots):
    dp_count = lax.axis_size("dp")
    mp_count = lax.axis_size("mp")
    dp_index = lax.axis_index("dp")
    partial_blocks = grad_partials[0]
    per_shard = partial_blocks.shape[0]
    width = partial_blocks.shape[2]
    rows = width // dp_count
    area = width * width
    cells = owner_lists.shape[0] * area
    piece = jax.ShapeDtypeStruct((rows, width), jnp.bfloat16)
    lanes = 128

    params = pltpu.CompilerParams(vmem_limit_bytes=16 * 2**20)

    def over_dp(factor):
        return lax.all_to_all(
            factor[0, 0].reshape(dp_count, rows, width), "dp", split_axis=0, concat_axis=0, tiled=True
        )

    plan = pl.pallas_call(
        functools.partial(plan_kernel, mp_count, per_shard),
        out_shape=jax.ShapeDtypeStruct((mp_count + per_shard,), jnp.int32),
        in_specs=[SMEM, SMEM],
        out_specs=SMEM,
        compiler_params=params,
    )(owner_lists, owner_offsets)
    right_slots = over_dp(right_roots)
    total = core_sum(partial_blocks, dp_index)
    right_slots, total, plan = lax.optimization_barrier((right_slots, total, plan))
    outgoing = pl.pallas_call(
        functools.partial(right_kernel, mp_count),
        out_shape=[piece] * mp_count,
        in_specs=[SMEM, VMEM],
        out_specs=[VMEM] * mp_count,
        compiler_params=params,
    )(plan, right_slots)
    left_slots = over_dp(left_roots)
    far = mp_count // 2
    middle = far + far // 2
    distant = [d for pair in zip(range(far, middle), range(middle, mp_count)) for d in pair]
    order = [1, distant[0], *range(2, far), *distant[1:]]
    right_arrived = [outgoing[0]] + [swap(outgoing[d], "mp", d) for d in order]
    total = chip_sum(total, dp_count, dp_index)
    total_f = total.astype(jnp.float32)
    half_sq = jnp.broadcast_to(
        jnp.sum(total_f * total_f, axis=(1, 2)).reshape(per_shard, 1),
        (per_shard, lanes),
    )
    left_outgoing = pl.pallas_call(
        functools.partial(left_kernel, mp_count),
        out_shape=jax.ShapeDtypeStruct((mp_count, rows * width // lanes + 16, lanes), jnp.bfloat16),
        in_specs=[SMEM, VMEM, VMEM],
        out_specs=VMEM,
        compiler_params=params,
    )(plan, left_slots, half_sq)
    left_arrived = lax.all_to_all(left_outgoing, "mp", split_axis=0, concat_axis=0, tiled=True)
    right_rows = pl.pallas_call(
        functools.partial(pick_kernel, mp_count, per_shard, [0] + order),
        out_shape=jax.ShapeDtypeStruct((per_shard, rows, width), jnp.bfloat16),
        in_specs=[SMEM] + [VMEM] * mp_count + [ANY],
        out_specs=VMEM,
        compiler_params=params,
    )(plan, *right_arrived, left_outgoing)
    right = gather_rows(right_rows, dp_count, dp_index)

    grad = whole_rows(total, dp_count, dp_index)
    right_prod = jnp.einsum(
        "bij,bjk->bik", grad, right, preferred_element_type=jnp.float32
    ).astype(jnp.bfloat16)
    precond, stats = pl.pallas_call(
        functools.partial(precond_kernel, mp_count, per_shard),
        out_shape=[
            jax.ShapeDtypeStruct((per_shard, rows, width), jnp.float32),
            jax.ShapeDtypeStruct((pl.cdiv(2 * per_shard + 1, 8) * 8, lanes), jnp.float32),
        ],
        in_specs=[SMEM, VMEM, VMEM, VMEM],
        out_specs=[VMEM, VMEM],
        scratch_shapes=[pltpu.VMEM((rows, width), jnp.bfloat16)],
        compiler_params=params,
    )(plan, right_prod, half_sq, left_arrived)
    parts = [stats] + [swap(stats, "dp", d) for d in range(1, dp_count)]
    return pl.pallas_call(
        functools.partial(finish_kernel, area, cells),
        out_shape=jax.ShapeDtypeStruct((per_shard, rows, width), jnp.bfloat16),
        in_specs=[VMEM] * (1 + dp_count),
        out_specs=VMEM,
        compiler_params=params,
    )(precond, *parts)


def solution(mesh):
    return jax.shard_map(
        shards,
        mesh=mesh,
        in_specs=(
            P("dp", "mp", None, None),
            P(),
            P(),
            P("mp", "dp", None, None),
            P("mp", "dp", None, None),
        ),
        out_specs=P("mp", "dp", None),
        check_vma=False,
    )
```

```python
import functools

import jax
import jax.numpy as jnp
from jax import lax
from jax.experimental import pallas as pl
from jax.experimental.pallas import tpu as pltpu
from jax.sharding import PartitionSpec as P

epsilon = 1e-06
max_rms = 1.0

SMEM = pl.BlockSpec(memory_space=pltpu.SMEM)
VMEM = pl.BlockSpec(memory_space=pltpu.VMEM)
ANY = pl.BlockSpec(memory_space=pl.ANY)


def swap(value, axis, distance):
    count = lax.axis_size(axis)
    return lax.ppermute(value, axis, [(i, i ^ distance) for i in range(count)])


def add_rounded(a, b):
    return (a.astype(jnp.float32) + b.astype(jnp.float32)).astype(jnp.bfloat16)


def core_sum(partial_blocks, dp_index):
    half = partial_blocks.shape[1] // 2
    core = dp_index % 2
    other = swap(partial_blocks, "dp", 1)
    kept = lax.dynamic_slice_in_dim(partial_blocks, core * half, half, axis=1)
    taken = lax.dynamic_slice_in_dim(other, core * half, half, axis=1)
    return add_rounded(kept, taken)


def chip_sum(total, dp_count, dp_index):
    distance = 2
    while distance < dp_count:
        part = total.shape[1] // 2
        bit = (dp_index // distance) % 2
        kept = lax.dynamic_slice_in_dim(total, bit * part, part, axis=1)
        given = lax.dynamic_slice_in_dim(total, (1 - bit) * part, part, axis=1)
        total = add_rounded(kept, swap(given, "dp", distance))
        distance *= 2
    return total


def whole_rows(total, dp_count, dp_index):
    part = total.shape[1]
    pieces, distance = {0: total}, dp_count // 2
    while distance >= 1:
        pieces |= {d ^ distance: swap(piece, "dp", distance) for d, piece in pieces.items()}
        distance //= 2
    whole = jnp.zeros((total.shape[0], part * dp_count, total.shape[2]), total.dtype)
    for d, piece in pieces.items():
        holder, place, distance = dp_index ^ d, 0, 1
        while distance < dp_count:
            place = 2 * place + (holder // distance) % 2
            distance *= 2
        whole = lax.dynamic_update_slice_in_dim(whole, piece, place * part, axis=1)
    return whole


def gather_rows(rows, dp_count, dp_index):
    per_shard, _, width = rows.shape
    parts = rows[:, None]
    distance = dp_count // 2
    while distance >= 1:
        other = swap(parts, "dp", distance)
        bit = (dp_index // distance) % 2
        low = jnp.where(bit == 0, parts, other)
        high = jnp.where(bit == 0, other, parts)
        parts = jnp.stack([low, high], axis=2)
        parts = parts.reshape(per_shard, -1, *rows.shape[1:])
        distance //= 2
    return parts.reshape(per_shard, -1, width)


def plan_kernel(mp_count, per_shard, lists, offsets, plan):
    column = lax.axis_index("mp")
    start = offsets[column]
    for j in range(mp_count):
        plan[j] = 0

    def note(p, carry):
        plan[lists[p] // per_shard] = p - start
        return carry

    lax.fori_loop(start, offsets[column + 1], note, 0)

    def owner(p, carry):
        block = lists[p]

        @pl.when(block // per_shard == column)
        def _():
            plan[mp_count + block % per_shard] = lax.fori_loop(
                0, mp_count, lambda c, total: total + (offsets[c + 1] <= p).astype(jnp.int32), 0
            )

        return carry

    lax.fori_loop(0, lists.shape[0], owner, 0)


def right_kernel(mp_count, plan, slots, *outs):
    column = lax.axis_index("mp")
    for d in range(mp_count):
        outs[d][...] = slots[plan[column ^ d]]


def left_kernel(mp_count, plan, slots, half_sq, out):
    rows = slots.shape[1]
    lanes = out.shape[2]
    total = jnp.sum(half_sq[...], axis=0, keepdims=True)
    first = total.astype(jnp.bfloat16).astype(jnp.float32)
    second = (total - first).astype(jnp.bfloat16).astype(jnp.float32)
    third = total - first - second
    row = lax.broadcasted_iota(jnp.int32, (16, lanes), 0)
    parts = jnp.where(row == 0, first, jnp.where(row == 1, second, jnp.where(row == 2, third, 0.0)))
    parts = parts.astype(jnp.bfloat16)
    for j in range(mp_count):
        slot = plan[j]
        for c in range(slots.shape[2] // lanes):
            out[j, c * rows : (c + 1) * rows, :] = slots[slot, :, c * lanes : (c + 1) * lanes]
        out[j, out.shape[1] - 16 :, :] = parts


def pick_kernel(mp_count, per_shard, order, plan, *refs):
    arrived, out = dict(zip(order, refs)), refs[-1]
    shard = lax.axis_index("mp")
    for r in range(per_shard):
        source = plan[mp_count + r] ^ shard
        for d in range(mp_count):

            @pl.when(source == d)
            def _(d=d, r=r):
                out[r] = arrived[d][...]


def precond_kernel(mp_count, per_shard, plan, right_prod, half_sq, arrived, precond, stats, left):
    rows, lanes = left.shape[0], arrived.shape[2]
    stats[...] = jnp.zeros_like(stats)
    stats[per_shard : 2 * per_shard, :] = half_sq[...]
    parts = jnp.sum(arrived[:, arrived.shape[1] - 16 :, :].astype(jnp.float32), axis=0)
    stats[2 * per_shard : 2 * per_shard + 1, :] = jnp.sum(parts, axis=0, keepdims=True)
    for r in range(per_shard):
        source = plan[mp_count + r]
        for c in range(left.shape[1] // lanes):
            left[:, c * lanes : (c + 1) * lanes] = arrived[source, c * rows : (c + 1) * rows, :]
        product = jnp.dot(left[...], right_prod[r], preferred_element_type=jnp.float32)
        precond[r] = product
        total = jnp.sum(jnp.sum(product * product, axis=1, keepdims=True), axis=0, keepdims=True)
        stats[r : r + 1, :] = jnp.broadcast_to(total, (1, lanes))


def finish_kernel(area, cells, precond, *refs):
    parts, update = refs[:-1], refs[-1]
    per_shard = update.shape[0]
    total = parts[0][...]
    for part in parts[1:]:
        total += part[...]
    precond_sq, block_sq = total[:per_shard], total[per_shard : 2 * per_shard]
    square_total = total[2 * per_shard : 2 * per_shard + 1]
    graft = jnp.sqrt(block_sq / area + epsilon) / jnp.sqrt(precond_sq / area + epsilon)
    scale = max_rms / jnp.sqrt(square_total / cells + epsilon) * graft
    for r in range(per_shard):
        update[r] = (scale[r : r + 1, :1] * precond[r]).astype(update.dtype)


def shards(grad_partials, owner_lists, owner_offsets, left_roots, right_roots):
    dp_count = lax.axis_size("dp")
    mp_count = lax.axis_size("mp")
    dp_index = lax.axis_index("dp")
    partial_blocks = grad_partials[0]
    per_shard = partial_blocks.shape[0]
    width = partial_blocks.shape[2]
    rows = width // dp_count
    area = width * width
    cells = owner_lists.shape[0] * area
    piece = jax.ShapeDtypeStruct((rows, width), jnp.bfloat16)
    lanes = 128

    params = pltpu.CompilerParams(vmem_limit_bytes=16 * 2**20)

    def over_dp(factor):
        return lax.all_to_all(
            factor[0, 0].reshape(dp_count, rows, width), "dp", split_axis=0, concat_axis=0, tiled=True
        )

    plan = pl.pallas_call(
        functools.partial(plan_kernel, mp_count, per_shard),
        out_shape=jax.ShapeDtypeStruct((mp_count + per_shard,), jnp.int32),
        in_specs=[SMEM, SMEM],
        out_specs=SMEM,
        compiler_params=params,
    )(owner_lists, owner_offsets)
    right_slots = over_dp(right_roots)
    total = core_sum(partial_blocks, dp_index)
    right_slots, total, plan = lax.optimization_barrier((right_slots, total, plan))
    outgoing = pl.pallas_call(
        functools.partial(right_kernel, mp_count),
        out_shape=[piece] * mp_count,
        in_specs=[SMEM, VMEM],
        out_specs=[VMEM] * mp_count,
        compiler_params=params,
    )(plan, right_slots)
    left_slots = over_dp(left_roots)
    far = mp_count // 2
    middle = far + far // 2
    distant = [d for pair in zip(range(middle, mp_count), range(far, middle)) for d in pair]
    order = [1, distant[0], *range(2, far), *distant[1:]]
    right_arrived = [outgoing[0]] + [swap(outgoing[d], "mp", d) for d in order]
    total = chip_sum(total, dp_count, dp_index)
    total_f = total.astype(jnp.float32)
    half_sq = jnp.broadcast_to(
        jnp.sum(total_f * total_f, axis=(1, 2)).reshape(per_shard, 1),
        (per_shard, lanes),
    )
    left_outgoing = pl.pallas_call(
        functools.partial(left_kernel, mp_count),
        out_shape=jax.ShapeDtypeStruct((mp_count, rows * width // lanes + 16, lanes), jnp.bfloat16),
        in_specs=[SMEM, VMEM, VMEM],
        out_specs=VMEM,
        compiler_params=params,
    )(plan, left_slots, half_sq)
    left_arrived = lax.all_to_all(left_outgoing, "mp", split_axis=0, concat_axis=0, tiled=True)
    right_rows = pl.pallas_call(
        functools.partial(pick_kernel, mp_count, per_shard, [0] + order),
        out_shape=jax.ShapeDtypeStruct((per_shard, rows, width), jnp.bfloat16),
        in_specs=[SMEM] + [VMEM] * mp_count + [ANY],
        out_specs=VMEM,
        compiler_params=params,
    )(plan, *right_arrived, left_outgoing)
    right = gather_rows(right_rows, dp_count, dp_index)

    grad = whole_rows(total, dp_count, dp_index)
    right_prod = jnp.einsum(
        "bij,bjk->bik", grad, right, preferred_element_type=jnp.float32
    ).astype(jnp.bfloat16)
    precond, stats = pl.pallas_call(
        functools.partial(precond_kernel, mp_count, per_shard),
        out_shape=[
            jax.ShapeDtypeStruct((per_shard, rows, width), jnp.float32),
            jax.ShapeDtypeStruct((pl.cdiv(2 * per_shard + 1, 8) * 8, lanes), jnp.float32),
        ],
        in_specs=[SMEM, VMEM, VMEM, VMEM],
        out_specs=[VMEM, VMEM],
        scratch_shapes=[pltpu.VMEM((rows, width), jnp.bfloat16)],
        compiler_params=params,
    )(plan, right_prod, half_sq, left_arrived)
    parts = [stats] + [swap(stats, "dp", d) for d in reversed(range(1, dp_count))]
    return pl.pallas_call(
        functools.partial(finish_kernel, area, cells),
        out_shape=jax.ShapeDtypeStruct((per_shard, rows, width), jnp.bfloat16),
        in_specs=[VMEM] * (1 + dp_count),
        out_specs=VMEM,
        compiler_params=params,
    )(precond, *parts)


def solution(mesh):
    return jax.shard_map(
        shards,
        mesh=mesh,
        in_specs=(
            P("dp", "mp", None, None),
            P(),
            P(),
            P("mp", "dp", None, None),
            P("mp", "dp", None, None),
        ),
        out_specs=P("mp", "dp", None),
        check_vma=False,
    )
```
